32 devices in a mesh: sub: 8 (over z, x), grp: 4 (over y, core).
Axes of the slice: x: 2, y: 2, z: 4, core: 2. Of those that a mesh axis runs over, the one named last changes fastest.
Arguments:
- right_side: float32 [65536, 128], P(('sub', 'grp')), may hold values from -6 to 6
- noise_var: float32 [65536], P(('sub', 'grp')), may hold values from 0.5 to 2
- near_tiles: bfloat16 [256, 6, 256, 256], P(('sub', 'grp')), may hold values from -0.15625 to 0.15625
- near_index: int32 [256, 6], P(('sub', 'grp')), may hold values from 0 to 255, as said below
- leaf_basis: bfloat16 [256, 64, 256], P(('sub', 'grp')), may hold values from -0.375 to 0.375
- leaf_transfer: bfloat16 [256, 64, 64], P(('sub', 'grp')), may hold values from -0.4375 to 0.4375
- leaf_coupling: bfloat16 [256, 4, 64, 64], P(('sub', 'grp')), may hold values from -0.375 to 0.375
- far_leaf: int32 [256, 4], P(('sub', 'grp')), may hold values from 0 to 255, as said below
- dev_transfer: bfloat16 [32, 64, 64], P(('sub', 'grp')), may hold values from -0.4375 to 0.4375
- dev_coupling: bfloat16 [32, 4, 64, 64], P(('sub', 'grp')), may hold values from -0.375 to 0.375
- far_dev: int32 [32, 4], P(('sub', 'grp')), may hold values from 0 to 31, as said below
- mid_coupling: bfloat16 [4, 3, 64, 64], P('grp'), may hold values from -0.4375 to 0.4375
- far_mid: int32 [4, 3], P('grp'), may hold values from 0 to 3, as said below
Outputs:
- solution: float32 [65536, 128], P(('sub', 'grp'))
The draws below stay inside these ranges and needn't reach their ends.
Inputs may be any that keep to these rules, and one draw needn't show every extreme that they name: `near_index`: row l lists 6 different leaves, l itself among them, each within 6 leaves of l in the periodic leaf order (leaf indices taken modulo 256). `far_leaf`: row l lists 4 different leaves within 6 leaves of l in the periodic leaf order, none of them in row l of near_index. `far_dev`: row d lists 4 different subtrees other than d, each of the same group as d. `far_mid`: row m lists 3 different mid nodes other than m.
All inputs are finite; a program needn't handle non-finite values.
Results may differ from the reference program's by a relative error of at most 0.025.
Values may be sent and summed in bfloat16 or wider, within the bound.
A program may use at most 64 MiB of HBM per device.

```python
import math
import jax
import jax.numpy as jnp
from jax import lax

LEAF = 256
RANK = 64
PROBES = 128
LEAVES_DEV = 8
NEAR = 6
FAR_LEAF = 4
SPAN = 6
FAR_DEV = 4
FAR_MID = 3
ITERS = 4
GROUPS = 4
GROUP_DEVS = 8
MID_GRP = 1
MIDS = 4
SUBTREES = 32
LEAVES = 256
ROWS = 65536


def leaf_lists(key):
    inner = jax.random.fold_in(key, 11)
    width = 2 * SPAN + 1
    scores = jax.random.randint(inner, (LEAVES, width), 0, 1 << 20) * 64 + jnp.arange(width, dtype=jnp.int32)[None, :]
    scores = scores.at[:, SPAN].set(-1)
    order = jnp.argsort(scores, axis=1, stable=True)[:, :NEAR + FAR_LEAF].astype(jnp.int32)
    offsets = order - SPAN
    leaf_ids = jnp.arange(LEAVES, dtype=jnp.int32)[:, None]
    return jnp.mod(leaf_ids + offsets, LEAVES).astype(jnp.int32)


def draw_near_index(key, part):
    return leaf_lists(key)[:, :NEAR]


def draw_far_leaf(key, part):
    return leaf_lists(key)[:, NEAR:]


def draw_far_dev(key, part):
    inner = jax.random.fold_in(key, 23)
    scores = jax.random.randint(inner, (SUBTREES, GROUP_DEVS), 0, 1 << 20) * 128 + jnp.arange(GROUP_DEVS, dtype=jnp.int32)[None, :]
    dev_ids = jnp.arange(SUBTREES, dtype=jnp.int32)
    within = dev_ids // GROUPS
    group_of = dev_ids % GROUPS
    columns = jnp.arange(GROUP_DEVS, dtype=jnp.int32)[None, :]
    scores = jnp.where(columns == within[:, None], 1 << 30, scores)
    forced = (within[:, None] == 0) & (columns == GROUP_DEVS - 1) | (within[:, None] == GROUP_DEVS - 1) & (columns == 0)
    scores = jnp.where(forced, -1, scores)
    order = jnp.argsort(scores, axis=1, stable=True)[:, :FAR_DEV].astype(jnp.int32)
    return (order * GROUPS + group_of[:, None]).astype(jnp.int32)


def draw_far_mid(key, part):
    inner = jax.random.fold_in(key, 37)
    scores = jax.random.randint(inner, (MIDS, MIDS), 0, 1 << 20) * 128 + jnp.arange(MIDS, dtype=jnp.int32)[None, :]
    mid_ids = jnp.arange(MIDS, dtype=jnp.int32)[:, None]
    columns = jnp.arange(MIDS, dtype=jnp.int32)[None, :]
    scores = jnp.where(columns == mid_ids, 1 << 30, scores)
    forced = (mid_ids == 0) & (columns == MIDS - 1) | (mid_ids == MIDS - 1) & (columns == 0)
    scores = jnp.where(forced, -1, scores)
    return jnp.argsort(scores, axis=1, stable=True)[:, :FAR_MID].astype(jnp.int32)


def shard_levels(key, extent, cuts, smallest, largest):
    level, own = 1.0, jax.random.fold_in(key, 6)
    for dim, blocks in cuts:
        heights = jnp.exp(jax.random.uniform(jax.random.fold_in(own, dim), (blocks,), jnp.float32, smallest / len(cuts), largest / len(cuts)))
        level = level * jnp.repeat(heights, extent[dim] // blocks).reshape([-1 if axis == dim else 1 for axis in range(len(extent))])
    return level


def noise(stream_key, dims, deviation, most, shards=(), kind=jnp.bfloat16):
    factor_of = shard_levels(stream_key, dims, shards, -0.22, 0.18) if shards else 1.0
    result = jax.random.normal(stream_key, dims, jnp.float32) * deviation * factor_of
    return jnp.minimum(jnp.maximum(result, -most), most).astype(kind)


def setup_inputs(seed: int = 0) -> dict:
    key_list = jax.random.split(jax.random.key(seed), 14)
    return {
        "right_side": noise(key_list[0], (ROWS, PROBES), 1.0, 6.0, ((0, 32),), jnp.float32),
        "noise_var": jnp.clip(jnp.exp(math.log(2.0) - 1.3862944 * jax.random.uniform(key_list[1], (ROWS,), jnp.float32) ** shard_levels(key_list[1], (ROWS,), ((0, 32),), -0.2, 0.2)), 0.5, 2.0),
        "near_tiles": noise(key_list[2], (LEAVES, NEAR, LEAF, LEAF), (LEAF * NEAR) ** -0.5, 0.15625, ((0, 32),)),
        "near_index": draw_near_index(jax.random.fold_in(key_list[13], 71), 0),
        "leaf_basis": noise(key_list[4], (LEAVES, RANK, LEAF), LEAF ** -0.5, 0.375, ((0, 32),)),
        "leaf_transfer": noise(key_list[5], (LEAVES, RANK, RANK), (3 * RANK) ** -0.5, 0.4375, ((0, 32),)),
        "leaf_coupling": noise(key_list[6], (LEAVES, FAR_LEAF, RANK, RANK), (RANK * FAR_LEAF) ** -0.5, 0.375, ((0, 32),)),
        "far_leaf": draw_far_leaf(jax.random.fold_in(key_list[13], 71), 0),
        "dev_transfer": noise(key_list[8], (SUBTREES, RANK, RANK), (3 * RANK) ** -0.5, 0.4375, ((0, 32),)),
        "dev_coupling": noise(key_list[9], (SUBTREES, FAR_DEV, RANK, RANK), (RANK * FAR_DEV) ** -0.5, 0.375, ((0, 32),)),
        "far_dev": draw_far_dev(jax.random.fold_in(key_list[13], 71), 0),
        "mid_coupling": noise(key_list[11], (MIDS, FAR_MID, RANK, RANK), (RANK * FAR_MID) ** -0.5, 0.4375, ((0, 4),)),
        "far_mid": draw_far_mid(jax.random.fold_in(key_list[13], 71), 0),
    }


relax_step = 0.3


def operate(iterate, noise_var, near_tiles, near_index, leaf_basis, leaf_transfer, leaf_coupling, far_leaf, dev_transfer, dev_coupling, far_dev, mid_coupling, far_mid):
    rounded = iterate.astype(jnp.bfloat16).reshape(LEAVES, LEAF, PROBES)
    basis32 = leaf_basis.astype(jnp.float32)
    ltrans32 = leaf_transfer.astype(jnp.float32)
    dtrans32 = dev_transfer.astype(jnp.float32)
    leaf_coef = jnp.einsum("lrj,ljp->lrp", basis32, rounded.astype(jnp.float32)).astype(jnp.bfloat16)
    dev_terms = jnp.einsum("lrs,lsp->lrp", ltrans32, leaf_coef.astype(jnp.float32))
    dev_coef = dev_terms.reshape(SUBTREES, LEAVES_DEV, RANK, PROBES).sum(1).astype(jnp.bfloat16)
    lifted = jnp.einsum("drs,dsp->drp", dtrans32, dev_coef.astype(jnp.float32)).astype(jnp.bfloat16)
    grouped = lifted.astype(jnp.float32).reshape(MID_GRP, 8, GROUPS, RANK, PROBES).sum(1)
    mid_coef = jnp.transpose(grouped, (1, 0, 2, 3)).reshape(MIDS, RANK, PROBES).astype(jnp.bfloat16)
    mid_field = jnp.einsum("mkrs,mksp->mrp", mid_coupling.astype(jnp.float32), mid_coef[far_mid].astype(jnp.float32)).astype(jnp.bfloat16)
    dev_ids = jnp.arange(SUBTREES, dtype=jnp.int32)
    parent = (dev_ids % GROUPS) * MID_GRP + (dev_ids // GROUPS) // 8
    dev_field = jnp.einsum("dkrs,dksp->drp", dev_coupling.astype(jnp.float32), dev_coef[far_dev].astype(jnp.float32))
    dev_field = dev_field + jnp.einsum("drs,drp->dsp", dtrans32, mid_field[parent].astype(jnp.float32))
    dev_field = dev_field.astype(jnp.bfloat16)
    spread = jnp.repeat(dev_field, LEAVES_DEV, axis=0).astype(jnp.float32)
    leaf_field = jnp.einsum("lkrs,lksp->lrp", leaf_coupling.astype(jnp.float32), leaf_coef[far_leaf].astype(jnp.float32))
    leaf_field = (leaf_field + jnp.einsum("lrs,lrp->lsp", ltrans32, spread)).astype(jnp.bfloat16)
    far_part = jnp.einsum("lrj,lrp->ljp", basis32, leaf_field.astype(jnp.float32))

    def near_block(pieces):
        tiles, indices = pieces
        gathered = rounded[indices].astype(jnp.float32)
        return jnp.einsum("lkij,lkjp->lip", tiles.astype(jnp.float32), gathered)

    near_part = lax.map(near_block, (near_tiles.reshape(SUBTREES, LEAVES_DEV, NEAR, LEAF, LEAF), near_index.reshape(SUBTREES, LEAVES_DEV, NEAR)))
    total = near_part.reshape(LEAVES, LEAF, PROBES) + far_part
    return total.reshape(ROWS, PROBES) + noise_var[:, None] * iterate


def reference(right_side, noise_var, near_tiles, near_index, leaf_basis, leaf_transfer, leaf_coupling, far_leaf, dev_transfer, dev_coupling, far_dev, mid_coupling, far_mid):
    iterate = relax_step * right_side
    for sweep in range(ITERS):
        image = operate(iterate, noise_var, near_tiles, near_index, leaf_basis, leaf_transfer, leaf_coupling, far_leaf, dev_transfer, dev_coupling, far_dev, mid_coupling, far_mid)
        iterate = iterate + relax_step * (right_side - image)
    return iterate
```

```python
import functools

import jax
import jax.numpy as jnp
from jax import lax
from jax.experimental import pallas as pl
from jax.experimental.pallas import tpu as pltpu
from jax.sharding import PartitionSpec as P

SPAN = 6
ITERS = 4
MID_DEVS = 8
MESH = pl.DeviceIdType.MESH


relax_step = 0.3


def dot(a, b):
    return jnp.dot(a, b, preferred_element_type=jnp.float32)


def flip(a):
    return a.astype(jnp.float32).T.astype(jnp.bfloat16)


def kernel(
    groups,
    group_devs,
    near_ref,
    far_ref,
    fdev_ref,
    fmid_ref,
    rhs_ref,
    noise_ref,
    basis_ref,
    lt_ref,
    lc_ref,
    dt_ref,
    dc_ref,
    mc_ref,
    tiles_hbm,
    x_ref,
    tiles,
    basis_t,
    lt_t,
    dt_t,
    cwin,
    nbasis,
    dt_all,
    *rest,
):
    wins, rest = rest[:ITERS], rest[ITERS:]
    gaths, rest = rest[:ITERS], rest[ITERS:]
    mids, rest = rest[:ITERS], rest[ITERS:]
    (
        tile_sem,
        halo_send,
        halo_recv,
        nb_send,
        nb_recv,
        dt_send,
        dt_recv,
        g_send,
        g_recv,
        m_send,
        m_recv,
    ) = rest
    leaves = rhs_ref.shape[0]
    near = near_ref.shape[1]
    nfar = far_ref.shape[1]
    nfdev = fdev_ref.shape[1]
    nfmid = fmid_ref.shape[1]
    mid_grp = group_devs // MID_DEVS
    count = groups * group_devs
    sub = lax.axis_index("sub")
    grp = lax.axis_index("grp")
    me = sub * groups + grp
    nxt = lax.rem(me + 1, count)
    prv = lax.rem(me + count - 1, count)
    next_id = (nxt // groups, lax.rem(nxt, groups))
    prev_id = (prv // groups, lax.rem(prv, groups))

    def sub_peer(j):
        return lax.rem(sub + j, group_devs)

    def grp_peer(j):
        return lax.rem(grp + j, groups)

    def tile_copy(l):
        return pltpu.make_async_copy(tiles_hbm.at[l], tiles.at[l], tile_sem.at[l])

    for l in range(leaves):
        tile_copy(l).start()

    def remote(src, dst, send, recv, device):
        return pltpu.make_async_remote_copy(
            src_ref=src,
            dst_ref=dst,
            send_sem=send,
            recv_sem=recv,
            device_id=device,
            device_id_type=MESH,
        )

    def to_prev(it, l):
        return remote(
            wins[it].at[SPAN + l],
            wins[it].at[SPAN + leaves + l],
            halo_send.at[it, 0, l],
            halo_recv.at[it, 0, l],
            prev_id,
        )

    def to_next(it, h):
        return remote(
            wins[it].at[leaves + h],
            wins[it].at[h],
            halo_send.at[it, 1, h],
            halo_recv.at[it, 1, h],
            next_id,
        )

    def basis_copy(side):
        if side == 0:
            src, dst, device = basis_ref.at[pl.ds(0, SPAN)], nbasis.at[pl.ds(SPAN, SPAN)], prev_id
        else:
            src, dst, device = (
                basis_ref.at[pl.ds(leaves - SPAN, SPAN)],
                nbasis.at[pl.ds(0, SPAN)],
                next_id,
            )
        return remote(src, dst, nb_send.at[side], nb_recv.at[side], device)

    def dt_copy(j, owner):
        return remote(
            dt_ref.at[0], dt_all.at[owner], dt_send.at[j], dt_recv.at[j], (sub_peer(j), grp)
        )

    def gath_copy(it, j, owner):
        block = gaths[it].at[owner]
        return remote(block, block, g_send.at[it, j], g_recv.at[it, j], (sub_peer(j), grp))

    def mid_copy(it, j, owner):
        block = mids[it].at[pl.ds(owner * mid_grp, mid_grp)]
        return remote(block, block, m_send.at[it, j], m_recv.at[it, j], (sub, grp_peer(j)))

    barrier = pltpu.get_barrier_semaphore()
    for device in (prev_id, next_id):
        pl.semaphore_signal(barrier, inc=1, device_id=device, device_id_type=MESH)
    for j in range(1, group_devs):
        pl.semaphore_signal(barrier, inc=1, device_id=(sub_peer(j), grp), device_id_type=MESH)
    for j in range(1, groups):
        pl.semaphore_signal(barrier, inc=1, device_id=(sub, grp_peer(j)), device_id_type=MESH)

    for l in range(leaves):
        start = relax_step * rhs_ref[l]
        x_ref[l] = start
        wins[0][SPAN + l] = start.astype(jnp.bfloat16)
    pl.semaphore_wait(barrier, 2 + (group_devs - 1) + (groups - 1))

    for j in range(1, group_devs):
        dt_copy(j, sub).start()
    for l in range(SPAN):
        to_prev(0, l).start()
        to_next(0, l).start()
    basis_copy(0).start()
    basis_copy(1).start()

    dt_all[sub] = dt_ref[0]
    dt_t[...] = flip(dt_ref[0])
    for l in range(leaves):
        basis_t[l] = flip(basis_ref[l])
        lt_t[l] = flip(lt_ref[l])

    for it in range(ITERS):
        win, gath, mid = wins[it], gaths[it], mids[it]
        total = None
        for l in range(leaves):
            coef = dot(basis_ref[l], win[SPAN + l]).astype(jnp.bfloat16)
            cwin[SPAN + l] = coef
            term = dot(lt_ref[l], coef)
            total = term if total is None else total + term
        gath[sub] = total.astype(jnp.bfloat16)
        for j in range(1, group_devs):
            gath_copy(it, j, sub).start()

        for j in range(1, group_devs):
            owner = lax.rem(sub + group_devs - j, group_devs)
            if it == 0:
                dt_copy(j, owner).wait_recv()
            gath_copy(it, j, owner).wait_recv()
        for m in range(mid_grp):
            lifted = None
            for s in range(MID_DEVS):
                place = m * MID_DEVS + s
                term = dot(dt_all[place], gath[place]).astype(jnp.bfloat16).astype(jnp.float32)
                lifted = term if lifted is None else lifted + term
            mid[grp * mid_grp + m] = lifted.astype(jnp.bfloat16)
        for j in range(1, groups):
            mid_copy(it, j, grp).start()

        dev_total = None
        for k in range(nfdev):
            term = dot(dc_ref[0, k], gath[fdev_ref[0, k]])
            dev_total = term if dev_total is None else dev_total + term
        for j in range(1, groups):
            owner = lax.rem(grp + groups - j, groups)
            mid_copy(it, j, owner).wait_recv()
        own_mid = sub // MID_DEVS
        field = None
        for k in range(nfmid):
            term = dot(mc_ref[own_mid, k], mid[fmid_ref[own_mid, k]])
            field = term if field is None else field + term
        dev_field = (dev_total + dot(dt_t[...], field.astype(jnp.bfloat16))).astype(jnp.bfloat16)

        if it == 0:
            basis_copy(0).wait_recv()
            basis_copy(1).wait_recv()
        for h in range(SPAN):
            to_prev(it, h).wait_recv()
            place = SPAN + leaves + h
            cwin[place] = dot(nbasis[SPAN + h], win[place]).astype(jnp.bfloat16)
            to_next(it, h).wait_recv()
            cwin[h] = dot(nbasis[h], win[h]).astype(jnp.bfloat16)

        def leaf_step(l, carry, it=it, win=win, dev_field=dev_field):
            if it == 0:
                tile_copy(l).wait()
            acc = dot(lt_t[l], dev_field)
            for k in range(nfar):
                acc = acc + dot(lc_ref[l, k], cwin[far_ref[l, k]])
            image = dot(basis_t[l], acc.astype(jnp.bfloat16))
            for k in range(near):
                image = image + dot(tiles[l, k], win[near_ref[l, k]])
            old = x_ref[l]
            image = image + noise_ref[l] * old
            new = old + relax_step * (rhs_ref[l] - image)
            x_ref[l] = new
            if it + 1 < ITERS:
                wins[it + 1][SPAN + l] = new.astype(jnp.bfloat16)

                @pl.when(l < SPAN)
                def _():
                    to_prev(it + 1, l).start()

                @pl.when(l >= leaves - SPAN)
                def _():
                    to_next(it + 1, l - (leaves - SPAN)).start()

            return carry

        lax.fori_loop(0, leaves, leaf_step, 0)

    for j in range(1, group_devs):
        dt_copy(j, sub).wait_send()
    basis_copy(0).wait_send()
    basis_copy(1).wait_send()
    for it in range(ITERS):
        for h in range(SPAN):
            to_prev(it, h).wait_send()
            to_next(it, h).wait_send()
        for j in range(1, group_devs):
            gath_copy(it, j, sub).wait_send()
        for j in range(1, groups):
            mid_copy(it, j, grp).wait_send()


def per_device(
    right_side,
    noise_var,
    near_tiles,
    near_index,
    leaf_basis,
    leaf_transfer,
    leaf_coupling,
    far_leaf,
    dev_transfer,
    dev_coupling,
    far_dev,
    mid_coupling,
    far_mid,
):
    leaves, near, size, _ = near_tiles.shape
    probes = right_side.shape[1]
    rank = leaf_basis.shape[1]
    groups = lax.axis_size("grp")
    group_devs = lax.axis_size("sub")
    total_leaves = leaves * groups * group_devs
    device = lax.axis_index("sub") * groups + lax.axis_index("grp")
    first_leaf = device * leaves
    near_local = jnp.mod(near_index - first_leaf + SPAN, total_leaves)
    far_local = jnp.mod(far_leaf - first_leaf + SPAN, total_leaves)
    far_within = far_dev // groups
    window = leaves + 2 * SPAN
    all_mids = groups * (group_devs // MID_DEVS)
    bf16 = jnp.bfloat16
    smem = pl.BlockSpec(memory_space=pltpu.SMEM)
    vmem = pl.BlockSpec(memory_space=pltpu.VMEM)
    dma = pltpu.SemaphoreType.DMA
    scratch = [
        pltpu.VMEM((leaves, near, size, size), bf16),
        pltpu.VMEM((leaves, size, rank), bf16),
        pltpu.VMEM((leaves, rank, rank), bf16),
        pltpu.VMEM((rank, rank), bf16),
        pltpu.VMEM((window, rank, probes), bf16),
        pltpu.VMEM((2 * SPAN, rank, size), bf16),
        pltpu.VMEM((group_devs, rank, rank), bf16),
    ]
    scratch += [pltpu.VMEM((window, size, probes), bf16)] * ITERS
    scratch += [pltpu.VMEM((group_devs, rank, probes), bf16)] * ITERS
    scratch += [pltpu.VMEM((all_mids, rank, probes), bf16)] * ITERS
    scratch += [
        dma((leaves,)),
        dma((ITERS, 2, SPAN)),
        dma((ITERS, 2, SPAN)),
        dma((2,)),
        dma((2,)),
        dma((group_devs,)),
        dma((group_devs,)),
        dma((ITERS, group_devs)),
        dma((ITERS, group_devs)),
        dma((ITERS, groups)),
        dma((ITERS, groups)),
    ]
    out = pl.pallas_call(
        functools.partial(kernel, groups, group_devs),
        out_shape=jax.ShapeDtypeStruct((leaves, size, probes), jnp.float32),
        in_specs=[smem] * 4 + [vmem] * 8 + [pl.BlockSpec(memory_space=pl.ANY)],
        out_specs=vmem,
        scratch_shapes=scratch,
        compiler_params=pltpu.CompilerParams(
            collective_id=0, has_side_effects=True, vmem_limit_bytes=48 * 1024 * 1024
        ),
    )(
        near_local,
        far_local,
        far_within,
        far_mid,
        right_side.reshape(leaves, size, probes),
        noise_var.reshape(leaves, size, 1),
        leaf_basis,
        leaf_transfer,
        leaf_coupling,
        dev_transfer,
        dev_coupling,
        mid_coupling,
        near_tiles,
    )
    return out.reshape(leaves * size, probes)


def solution(mesh):
    return jax.shard_map(
        per_device,
        mesh=mesh,
        in_specs=(
            P(("sub", "grp"), None),
            P(("sub", "grp")),
            P(("sub", "grp"), None, None, None),
            P(("sub", "grp"), None),
            P(("sub", "grp"), None, None),
            P(("sub", "grp"), None, None),
            P(("sub", "grp"), None, None, None),
            P(("sub", "grp"), None),
            P(("sub", "grp"), None, None),
            P(("sub", "grp"), None, None, None),
            P(("sub", "grp"), None),
            P("grp", None, None, None),
            P("grp", None),
        ),
        out_specs=P(("sub", "grp"), None),
        check_vma=False,
    )
```

```python
import functools

import jax
import jax.numpy as jnp
from jax import lax
from jax.experimental import pallas as pl
from jax.experimental.pallas import tpu as pltpu
from jax.sharding import PartitionSpec as P

SPAN = 6
ITERS = 4
MID_DEVS = 8
MESH = pl.DeviceIdType.MESH


relax_step = 0.3


def dot(a, b):
    return jnp.dot(a, b, preferred_element_type=jnp.float32)


def flip(a):
    return a.astype(jnp.float32).T.astype(jnp.bfloat16)


def kernel(
    groups,
    group_devs,
    near_hbm,
    far_hbm,
    fdev_hbm,
    fmid_hbm,
    rhs_hbm,
    noise_hbm,
    basis_hbm,
    lt_hbm,
    lc_hbm,
    dt_hbm,
    dc_hbm,
    mc_hbm,
    tiles_hbm,
    x_ref,
    near_raw,
    far_raw,
    fdev_ref,
    fmid_ref,
    near_ref,
    far_ref,
    rhs_ref,
    noise_raw,
    basis_ref,
    lt_ref,
    lc_ref,
    dt_ref,
    dc_ref,
    mc_ref,
    tiles,
    noise_ref,
    basis_t,
    lt_t,
    dt_t,
    cwin,
    nbasis,
    dt_all,
    gath_here,
    mid_here,
    image_ref,
    win,
    out,
    inc,
    gath,
    mid,
    in_sem,
    tile_sem,
    halo_send,
    halo_recv,
    nb_send,
    nb_recv,
    dt_send,
    dt_recv,
    g_send,
    g_recv,
    m_send,
    m_recv,
):
    leaves, size, probes = rhs_ref.shape
    near = near_ref.shape[1]
    nfar = far_ref.shape[0]
    nfdev = fdev_ref.shape[1]
    nfmid = fmid_ref.shape[1]
    mid_grp = group_devs // MID_DEVS
    count = groups * group_devs
    sub = lax.axis_index("sub")
    grp = lax.axis_index("grp")
    me = sub * groups + grp
    nxt = lax.rem(me + 1, count)
    prv = lax.rem(me + count - 1, count)
    next_id = (nxt // groups, lax.rem(nxt, groups))
    prev_id = (prv // groups, lax.rem(prv, groups))

    operands = [
        (rhs_hbm, rhs_ref),
        (basis_hbm, basis_ref),
        (dt_hbm, dt_ref),
        (lt_hbm, lt_ref),
        (near_hbm, near_raw),
        (far_hbm, far_raw),
        (fdev_hbm, fdev_ref),
        (fmid_hbm, fmid_ref),
        (noise_hbm, noise_raw),
        (lc_hbm, lc_ref),
        (dc_hbm, dc_ref),
        (mc_hbm, mc_ref),
    ]
    loads = [
        pltpu.make_async_copy(src, dst, in_sem.at[i]) for i, (src, dst) in enumerate(operands)
    ]
    for load in loads:
        load.start()
    tile_loads = [
        pltpu.make_async_copy(tiles_hbm.at[l], tiles.at[l], tile_sem.at[l]) for l in range(leaves)
    ]
    for load in tile_loads:
        load.start()

    def sub_peer(j):
        return lax.rem(sub + j, group_devs)

    def grp_peer(j):
        return lax.rem(grp + j, groups)

    def remote(src, dst, send, recv, device):
        return pltpu.make_async_remote_copy(
            src_ref=src,
            dst_ref=dst,
            send_sem=send,
            recv_sem=recv,
            device_id=device,
            device_id_type=MESH,
        )

    def to_prev(it, h):
        return remote(
            out.at[it, h],
            inc.at[it, SPAN + h],
            halo_send.at[it, 0, h],
            halo_recv.at[it, 0, h],
            prev_id,
        )

    def to_next(it, h):
        return remote(
            out.at[it, leaves - SPAN + h],
            inc.at[it, h],
            halo_send.at[it, 1, h],
            halo_recv.at[it, 1, h],
            next_id,
        )

    def basis_copy(side):
        if side == 0:
            src, dst, device = basis_ref.at[pl.ds(0, SPAN)], nbasis.at[pl.ds(SPAN, SPAN)], prev_id
        else:
            src, dst, device = (
                basis_ref.at[pl.ds(leaves - SPAN, SPAN)],
                nbasis.at[pl.ds(0, SPAN)],
                next_id,
            )
        return remote(src, dst, nb_send.at[side], nb_recv.at[side], device)

    def dt_copy(j, owner):
        return remote(
            dt_ref.at[0], dt_all.at[owner], dt_send.at[j], dt_recv.at[j], (sub_peer(j), grp)
        )

    def gath_copy(it, j, owner):
        block = gath.at[it, owner]
        return remote(block, block, g_send.at[it, j], g_recv.at[it, j], (sub_peer(j), grp))

    def mid_copy(it, j, owner):
        block = mid.at[it, pl.ds(owner * mid_grp, mid_grp)]
        return remote(block, block, m_send.at[it, j], m_recv.at[it, j], (sub, grp_peer(j)))

    early = SPAN // 2
    middle = early + 1
    prev_order = list(range(SPAN))
    next_order = list(range(SPAN - 1, -1, -1))
    prev_early, next_early = prev_order[:early], next_order[:early]
    ready = [
        l
        for l in range(leaves)
        if l >= SPAN - middle and l + SPAN - leaves < middle
    ]
    first = [h for h in range(SPAN) if h in prev_early]
    last = [leaves - SPAN + h for h in next_early]
    order = []
    for pair in zip(reversed(first), reversed(last)):
        order += [l for l in pair if l not in order]
    order += [l for l in range(leaves) if l not in order]

    def stage(it, step):
        h = next_order[step]
        to_next(it, h).wait_recv()
        block = inc[it, h]
        win[h] = block
        cwin[h] = dot(nbasis[h], block).astype(jnp.bfloat16)
        h = prev_order[step]
        to_prev(it, h).wait_recv()
        block = inc[it, SPAN + h]
        win[SPAN + leaves + h] = block
        cwin[SPAN + leaves + h] = dot(nbasis[SPAN + h], block).astype(jnp.bfloat16)

    def near_part(l):
        image = dot(tiles[l, 0], win[near_ref[l, 0]])
        for k in range(1, near):
            image = image + dot(tiles[l, k], win[near_ref[l, k]])
        return image

    barrier = pltpu.get_barrier_semaphore()
    for device in (prev_id, next_id):
        pl.semaphore_signal(barrier, inc=1, device_id=device, device_id_type=MESH)
    for j in range(1, group_devs):
        pl.semaphore_signal(barrier, inc=1, device_id=(sub_peer(j), grp), device_id_type=MESH)
    for j in range(1, groups):
        pl.semaphore_signal(barrier, inc=1, device_id=(sub, grp_peer(j)), device_id_type=MESH)

    loads[0].wait()
    for l in range(leaves):
        start = relax_step * rhs_ref[l]
        x_ref[l] = start
        out[0, l] = start.astype(jnp.bfloat16)
    pl.semaphore_wait(barrier, 2 + (group_devs - 1) + (groups - 1))

    for h in prev_early:
        to_prev(0, h).start()
    for h in next_early:
        to_next(0, h).start()
    for load in loads[1:]:
        load.wait()
    for j in range(1, group_devs):
        dt_copy(j, sub).start()
    basis_copy(0).start()
    basis_copy(1).start()

    total_leaves = leaves * count
    window = leaves + 2 * SPAN
    for l in range(leaves):
        for k in range(near):
            place = near_raw[l, k] - me * leaves + SPAN
            place = jnp.where(place < 0, place + total_leaves, place)
            place = jnp.where(place >= total_leaves, place - total_leaves, place)
            near_ref[l, k] = jnp.minimum(place, window - 1)
        for k in range(nfar):
            place = far_raw[k, l] - me * leaves + SPAN
            place = jnp.where(place < 0, place + total_leaves, place)
            place = jnp.where(place >= total_leaves, place - total_leaves, place)
            far_ref[k, l] = jnp.minimum(place, window - 1)

    dt_all[sub] = dt_ref[0]
    dt_t[...] = flip(dt_ref[0])
    lanes = noise_raw.shape[1]
    pieces = size // lanes
    for l in range(leaves):
        basis_t[l] = flip(basis_ref[l])
        lt_t[l] = flip(lt_ref[l])
        for c in range(pieces):
            row = noise_raw[pl.ds(l * pieces + c, 1), :]
            noise_ref[l, pl.ds(c * lanes, lanes), :] = jnp.broadcast_to(row, (probes, lanes)).T
    for j in range(1, group_devs):
        dt_copy(j, lax.rem(sub + group_devs - j, group_devs)).wait_recv()
    for load in tile_loads:
        load.wait()

    def sweep(it, carry):
        total = None
        for l in range(leaves):
            block = out[it, l]
            win[SPAN + l] = block
            coef = dot(basis_ref[l], block).astype(jnp.bfloat16)
            cwin[SPAN + l] = coef
            term = dot(lt_ref[l], coef)
            total = term if total is None else total + term
        gath[it, sub] = total.astype(jnp.bfloat16)
        for j in range(1, group_devs):
            gath_copy(it, j, sub).start()
        for step in range(early, middle):
            to_prev(it, prev_order[step]).start()
            to_next(it, next_order[step]).start()

        for j in range(1, group_devs):
            gath_copy(it, j, lax.rem(sub + group_devs - j, group_devs)).wait_recv()
        for m in range(mid_grp):
            lifted = None
            for s in range(MID_DEVS):
                place = m * MID_DEVS + s
                coef = gath[it, place]
                gath_here[place] = coef
                term = dot(dt_all[place], coef).astype(jnp.bfloat16).astype(jnp.float32)
                lifted = term if lifted is None else lifted + term
            mid[it, grp * mid_grp + m] = lifted.astype(jnp.bfloat16)
        for j in range(1, groups):
            mid_copy(it, j, grp).start()
        for step in range(middle, SPAN):
            to_prev(it, prev_order[step]).start()
            to_next(it, next_order[step]).start()

        dev_total = None
        for k in range(nfdev):
            term = dot(dc_ref[0, k], gath_here[lax.div(fdev_ref[0, k], groups)])
            dev_total = term if dev_total is None else dev_total + term

        @pl.when(it == 0)
        def _():
            basis_copy(0).wait_recv()
            basis_copy(1).wait_recv()

        for step in range(middle):
            stage(it, step)
        for l in ready:
            image_ref[l] = near_part(l)

        for j in range(1, groups):
            mid_copy(it, j, lax.rem(grp + groups - j, groups)).wait_recv()
        for m in range(groups * mid_grp):
            mid_here[m] = mid[it, m]
        own_mid = sub // MID_DEVS
        field = None
        for k in range(nfmid):
            term = dot(mc_ref[own_mid, k], mid_here[fmid_ref[own_mid, k]])
            field = term if field is None else field + term
        dev_field = (dev_total + dot(dt_t[...], field.astype(jnp.bfloat16))).astype(jnp.bfloat16)

        for step in range(middle, SPAN):
            stage(it, step)

        for l in order:
            acc = dot(lt_t[l], dev_field)
            for k in range(nfar):
                acc = acc + dot(lc_ref[l, k], cwin[far_ref[k, l]])
            image = image_ref[l] if l in ready else near_part(l)
            image = image + dot(basis_t[l], acc.astype(jnp.bfloat16))
            old = x_ref[l]
            image = image + noise_ref[l] * old
            new = old + relax_step * (rhs_ref[l] - image)
            x_ref[l] = new

            @pl.when(it + 1 < ITERS)
            def _():
                out[it + 1, l] = new.astype(jnp.bfloat16)
                if l in first:
                    to_prev(it + 1, l).start()
                if l in last:
                    to_next(it + 1, l - (leaves - SPAN)).start()

        return carry

    lax.fori_loop(0, ITERS, sweep, 0)

    for j in range(1, group_devs):
        dt_copy(j, sub).wait_send()
    basis_copy(0).wait_send()
    basis_copy(1).wait_send()

    def drain(it, carry):
        for h in range(SPAN):
            to_prev(it, h).wait_send()
            to_next(it, h).wait_send()
        for j in range(1, group_devs):
            gath_copy(it, j, sub).wait_send()
        for j in range(1, groups):
            mid_copy(it, j, grp).wait_send()
        return carry

    lax.fori_loop(0, ITERS, drain, 0)


def per_device(
    right_side,
    noise_var,
    near_tiles,
    near_index,
    leaf_basis,
    leaf_transfer,
    leaf_coupling,
    far_leaf,
    dev_transfer,
    dev_coupling,
    far_dev,
    mid_coupling,
    far_mid,
):
    leaves, near, size, _ = near_tiles.shape
    probes = right_side.shape[1]
    rank = leaf_basis.shape[1]
    groups = lax.axis_size("grp")
    group_devs = lax.axis_size("sub")
    window = leaves + 2 * SPAN
    all_mids = groups * (group_devs // MID_DEVS)
    bf16, f32, i32 = jnp.bfloat16, jnp.float32, jnp.int32
    dma = pltpu.SemaphoreType.DMA
    operands = [
        near_index,
        far_leaf.T,
        far_dev,
        far_mid,
        right_side.reshape(leaves, size, probes),
        noise_var.reshape(-1, probes),
        leaf_basis,
        leaf_transfer,
        leaf_coupling,
        dev_transfer,
        dev_coupling,
        mid_coupling,
        near_tiles,
    ]
    scratch = [pltpu.SMEM(a.shape, i32) for a in operands[:4]]
    scratch += [pltpu.SMEM(a.shape, i32) for a in operands[:2]]
    scratch += [pltpu.VMEM(a.shape, a.dtype) for a in operands[4:]]
    scratch += [
        pltpu.VMEM((leaves, size, probes), f32),
        pltpu.VMEM((leaves, size, rank), bf16),
        pltpu.VMEM((leaves, rank, rank), bf16),
        pltpu.VMEM((rank, rank), bf16),
        pltpu.VMEM((window, rank, probes), bf16),
        pltpu.VMEM((2 * SPAN, rank, size), bf16),
        pltpu.VMEM((group_devs, rank, rank), bf16),
        pltpu.VMEM((group_devs, rank, probes), bf16),
        pltpu.VMEM((all_mids, rank, probes), bf16),
        pltpu.VMEM((leaves, size, probes), f32),
        pltpu.VMEM((window, size, probes), bf16),
        pltpu.VMEM((ITERS, leaves, size, probes), bf16),
        pltpu.VMEM((ITERS, 2 * SPAN, size, probes), bf16),
        pltpu.VMEM((ITERS, group_devs, rank, probes), bf16),
        pltpu.VMEM((ITERS, all_mids, rank, probes), bf16),
        dma((12,)),
        dma((leaves,)),
        dma((ITERS, 2, SPAN)),
        dma((ITERS, 2, SPAN)),
        dma((2,)),
        dma((2,)),
        dma((group_devs,)),
        dma((group_devs,)),
        dma((ITERS, group_devs)),
        dma((ITERS, group_devs)),
        dma((ITERS, groups)),
        dma((ITERS, groups)),
    ]
    result = pl.pallas_call(
        functools.partial(kernel, groups, group_devs),
        out_shape=jax.ShapeDtypeStruct((leaves, size, probes), f32),
        in_specs=[pl.BlockSpec(memory_space=pl.ANY)] * len(operands),
        out_specs=pl.BlockSpec(memory_space=pltpu.VMEM),
        scratch_shapes=scratch,
        compiler_params=pltpu.CompilerParams(
            collective_id=0, has_side_effects=True, vmem_limit_bytes=56 * 1024 * 1024
        ),
    )(*operands)
    return result.reshape(leaves * size, probes)


def solution(mesh):
    return jax.shard_map(
        per_device,
        mesh=mesh,
        in_specs=(
            P(("sub", "grp"), None),
            P(("sub", "grp")),
            P(("sub", "grp"), None, None, None),
            P(("sub", "grp"), None),
            P(("sub", "grp"), None, None),
            P(("sub", "grp"), None, None),
            P(("sub", "grp"), None, None, None),
            P(("sub", "grp"), None),
            P(("sub", "grp"), None, None),
            P(("sub", "grp"), None, None, None),
            P(("sub", "grp"), None),
            P("grp", None, None, None),
            P("grp", None),
        ),
        out_specs=P(("sub", "grp"), None),
        check_vma=False,
    )
```

```python
import functools

import jax
import jax.numpy as jnp
from jax import lax
from jax.experimental import pallas as pl
from jax.experimental.pallas import tpu as pltpu
from jax.sharding import PartitionSpec as P

SPAN = 6
ITERS = 4
MID_DEVS = 8
MESH = pl.DeviceIdType.MESH


relax_step = 0.3


def dot(a, b):
    return jnp.dot(a, b, preferred_element_type=jnp.float32)


def flip(a):
    return a.astype(jnp.float32).T.astype(jnp.bfloat16)


def kernel(
    groups,
    group_devs,
    near_hbm,
    far_hbm,
    fdev_hbm,
    fmid_hbm,
    rhs_hbm,
    noise_hbm,
    basis_hbm,
    lt_hbm,
    lc_hbm,
    dt_hbm,
    dc_hbm,
    mc_hbm,
    tiles_hbm,
    x_ref,
    near_raw,
    far_raw,
    fdev_ref,
    fmid_ref,
    near_ref,
    far_ref,
    rhs_ref,
    noise_raw,
    basis_ref,
    lt_ref,
    lc_ref,
    dt_ref,
    dc_ref,
    mc_ref,
    tiles,
    noise_ref,
    basis_t,
    far_all,
    field_ref,
    dt_t,
    cwin,
    nbasis,
    dt_all,
    gath_here,
    mid_here,
    image_ref,
    win,
    out,
    inc,
    gath,
    mid,
    in_sem,
    tile_sem,
    halo_send,
    halo_recv,
    nb_send,
    nb_recv,
    dt_send,
    dt_recv,
    g_send,
    g_recv,
    m_send,
    m_recv,
):
    leaves, size, probes = rhs_ref.shape
    rank = basis_ref.shape[1]
    near = near_ref.shape[1]
    nfar = far_ref.shape[0]
    nfdev = fdev_ref.shape[1]
    nfmid = fmid_ref.shape[1]
    mid_grp = group_devs // MID_DEVS
    count = groups * group_devs
    sub = lax.axis_index("sub")
    grp = lax.axis_index("grp")
    me = sub * groups + grp
    nxt = lax.rem(me + 1, count)
    prv = lax.rem(me + count - 1, count)
    next_id = (nxt // groups, lax.rem(nxt, groups))
    prev_id = (prv // groups, lax.rem(prv, groups))

    operands = [
        (rhs_hbm, rhs_ref),
        (basis_hbm, basis_ref),
        (dt_hbm, dt_ref),
        (lt_hbm, lt_ref),
        (near_hbm, near_raw),
        (far_hbm, far_raw),
        (fdev_hbm, fdev_ref),
        (fmid_hbm, fmid_ref),
        (noise_hbm, noise_raw),
        (lc_hbm, lc_ref),
        (dc_hbm, dc_ref),
        (mc_hbm, mc_ref),
    ]
    loads = [
        pltpu.make_async_copy(src, dst, in_sem.at[i]) for i, (src, dst) in enumerate(operands)
    ]
    for load in loads:
        load.start()
    tile_loads = [
        pltpu.make_async_copy(tiles_hbm.at[l], tiles.at[l], tile_sem.at[l]) for l in range(leaves)
    ]
    for load in tile_loads:
        load.start()

    def sub_peer(j):
        return lax.rem(sub + j, group_devs)

    def grp_peer(j):
        return lax.rem(grp + j, groups)

    def remote(src, dst, send, recv, device):
        return pltpu.make_async_remote_copy(
            src_ref=src,
            dst_ref=dst,
            send_sem=send,
            recv_sem=recv,
            device_id=device,
            device_id_type=MESH,
        )

    def to_prev(it, h):
        return remote(
            out.at[it, h],
            inc.at[it, SPAN + h],
            halo_send.at[it, 0, h],
            halo_recv.at[it, 0, h],
            prev_id,
        )

    def to_next(it, h):
        return remote(
            out.at[it, leaves - SPAN + h],
            inc.at[it, h],
            halo_send.at[it, 1, h],
            halo_recv.at[it, 1, h],
            next_id,
        )

    def basis_copy(side):
        if side == 0:
            src, dst, device = basis_ref.at[pl.ds(0, SPAN)], nbasis.at[pl.ds(SPAN, SPAN)], prev_id
        else:
            src, dst, device = (
                basis_ref.at[pl.ds(leaves - SPAN, SPAN)],
                nbasis.at[pl.ds(0, SPAN)],
                next_id,
            )
        return remote(src, dst, nb_send.at[side], nb_recv.at[side], device)

    def dt_copy(j, owner):
        return remote(
            dt_ref.at[0], dt_all.at[owner], dt_send.at[j], dt_recv.at[j], (sub_peer(j), grp)
        )

    def gath_copy(it, j, owner):
        block = gath.at[it, owner]
        return remote(block, block, g_send.at[it, j], g_recv.at[it, j], (sub_peer(j), grp))

    def mid_copy(it, j, owner):
        block = mid.at[it, pl.ds(owner * mid_grp, mid_grp)]
        return remote(block, block, m_send.at[it, j], m_recv.at[it, j], (sub, grp_peer(j)))

    early = SPAN // 2
    middle = SPAN - 1
    prev_order = list(range(SPAN))
    next_order = list(range(SPAN - 1, -1, -1))
    first = prev_order[:early]
    last = [leaves - SPAN + h for h in next_order[:early]]

    def steps_needed(l):
        return min(SPAN, max(0, SPAN - l, l + SPAN - leaves + 1))

    by_step = [[l for l in range(leaves) if steps_needed(l) == n] for n in range(SPAN + 1)]

    def sends_first(batch):
        return sorted(batch, key=lambda l: (l not in first and l not in last, l))

    def stage(it, step):
        h = next_order[step]
        to_next(it, h).wait_recv()
        block = inc[it, h]
        win[h] = block
        cwin[h] = dot(nbasis[h], block).astype(jnp.bfloat16)
        h = prev_order[step]
        to_prev(it, h).wait_recv()
        block = inc[it, SPAN + h]
        win[SPAN + leaves + h] = block
        cwin[SPAN + leaves + h] = dot(nbasis[SPAN + h], block).astype(jnp.bfloat16)

    def near_part(l):
        image = dot(tiles[l, 0], win[near_ref[l, 0]])
        for k in range(1, near):
            image = image + dot(tiles[l, k], win[near_ref[l, k]])
        return image

    barrier = pltpu.get_barrier_semaphore()
    for device in (prev_id, next_id):
        pl.semaphore_signal(barrier, inc=1, device_id=device, device_id_type=MESH)
    for j in range(1, group_devs):
        pl.semaphore_signal(barrier, inc=1, device_id=(sub_peer(j), grp), device_id_type=MESH)
    for j in range(1, groups):
        pl.semaphore_signal(barrier, inc=1, device_id=(sub, grp_peer(j)), device_id_type=MESH)

    loads[0].wait()
    for l in range(leaves):
        start = relax_step * rhs_ref[l]
        x_ref[l] = start
        out[0, l] = start.astype(jnp.bfloat16)
    pl.semaphore_wait(barrier, 2 + (group_devs - 1) + (groups - 1))

    for step in range(early):
        to_prev(0, prev_order[step]).start()
        to_next(0, next_order[step]).start()
    for load in loads[1:]:
        load.wait()
    for j in range(1, group_devs):
        dt_copy(j, sub).start()
    basis_copy(0).start()
    basis_copy(1).start()

    total_leaves = leaves * count
    window = leaves + 2 * SPAN
    for l in range(leaves):
        for k in range(near):
            place = near_raw[l, k] - me * leaves + SPAN
            place = jnp.where(place < 0, place + total_leaves, place)
            place = jnp.where(place >= total_leaves, place - total_leaves, place)
            near_ref[l, k] = jnp.minimum(place, window - 1)
        for k in range(nfar):
            place = far_raw[k, l] - me * leaves + SPAN
            place = jnp.where(place < 0, place + total_leaves, place)
            place = jnp.where(place >= total_leaves, place - total_leaves, place)
            far_ref[k, l] = jnp.minimum(place, window - 1)

    dt_all[sub] = dt_ref[0]
    dt_t[...] = flip(dt_ref[0])
    lanes = noise_raw.shape[1]
    pieces = size // lanes
    for l in range(leaves):
        basis_t[l] = flip(basis_ref[l])
        for k in range(nfar):
            far_all[l, :, pl.ds(k * rank, rank)] = lc_ref[l, k]
        far_all[l, :, pl.ds(nfar * rank, rank)] = flip(lt_ref[l])
        for c in range(pieces):
            row = noise_raw[pl.ds(l * pieces + c, 1), :]
            noise_ref[l, pl.ds(c * lanes, lanes), :] = jnp.broadcast_to(row, (probes, lanes)).T
    for j in range(1, group_devs):
        dt_copy(j, lax.rem(sub + group_devs - j, group_devs)).wait_recv()
    for load in tile_loads:
        load.wait()

    def sweep(it, carry):
        total = None
        for l in range(leaves):
            block = out[it, l]
            win[SPAN + l] = block
            coef = dot(basis_ref[l], block).astype(jnp.bfloat16)
            cwin[SPAN + l] = coef
            term = dot(lt_ref[l], coef)
            total = term if total is None else total + term
        gath[it, sub] = total.astype(jnp.bfloat16)
        for j in range(1, group_devs):
            gath_copy(it, j, sub).start()
        for step in range(early, middle):
            to_prev(it, prev_order[step]).start()
            to_next(it, next_order[step]).start()

        @pl.when(it == 0)
        def _():
            basis_copy(0).wait_recv()
            basis_copy(1).wait_recv()

        def arrive(steps):
            for step in steps:
                if step < SPAN:
                    stage(it, step)
            for step in steps:
                for l in by_step[step + 1]:
                    image_ref[l] = near_part(l)

        for l in by_step[0]:
            image_ref[l] = near_part(l)
        arrive(range(early))

        for j in range(1, group_devs):
            gath_copy(it, j, lax.rem(sub + group_devs - j, group_devs)).wait_recv()
        for m in range(mid_grp):
            lifted = None
            for s in range(MID_DEVS):
                place = m * MID_DEVS + s
                coef = gath[it, place]
                gath_here[place] = coef
                term = dot(dt_all[place], coef).astype(jnp.bfloat16).astype(jnp.float32)
                lifted = term if lifted is None else lifted + term
            mid[it, grp * mid_grp + m] = lifted.astype(jnp.bfloat16)
        for j in range(1, groups):
            mid_copy(it, j, grp).start()
        for step in range(middle, SPAN):
            to_prev(it, prev_order[step]).start()
            to_next(it, next_order[step]).start()

        dev_total = None
        for k in range(nfdev):
            term = dot(dc_ref[0, k], gath_here[lax.div(fdev_ref[0, k], groups)])
            dev_total = term if dev_total is None else dev_total + term

        arrive(range(early, middle))

        for j in range(1, groups):
            mid_copy(it, j, lax.rem(grp + groups - j, groups)).wait_recv()
        for m in range(groups * mid_grp):
            mid_here[m] = mid[it, m]
        own_mid = sub // MID_DEVS
        field = None
        for k in range(nfmid):
            term = dot(mc_ref[own_mid, k], mid_here[fmid_ref[own_mid, k]])
            field = term if field is None else field + term
        dev_field = (dev_total + dot(dt_t[...], field.astype(jnp.bfloat16))).astype(jnp.bfloat16)

        def finish(batch):
            for l in batch:
                parts = [cwin[far_ref[k, l]] for k in range(nfar)] + [dev_field]
                field_ref[l] = dot(far_all[l], jnp.concatenate(parts, axis=0)).astype(jnp.bfloat16)
            for at in range(0, len(batch), 2):
                pair = batch[at : at + 2]
                for l in pair:
                    image = image_ref[l] + dot(basis_t[l], field_ref[l])
                    old = x_ref[l]
                    image = image + noise_ref[l] * old
                    new = old + relax_step * (rhs_ref[l] - image)
                    x_ref[l] = new
                    out[it + 1, l] = new.astype(jnp.bfloat16)
                if any(l in first or l in last for l in pair):

                    @pl.when(it + 1 < ITERS)
                    def _():
                        for l in pair:
                            if l in first:
                                to_prev(it + 1, l).start()
                            if l in last:
                                to_next(it + 1, l - (leaves - SPAN)).start()

        done = [l for step in range(middle + 1) for l in reversed(by_step[step])]
        finish(sends_first(done))
        arrive(range(middle, SPAN))
        finish(sends_first([l for l in range(leaves) if l not in done]))
        return carry

    lax.fori_loop(0, ITERS, sweep, 0)

    for j in range(1, group_devs):
        dt_copy(j, sub).wait_send()
    basis_copy(0).wait_send()
    basis_copy(1).wait_send()

    def drain(it, carry):
        for h in range(SPAN):
            to_prev(it, h).wait_send()
            to_next(it, h).wait_send()
        for j in range(1, group_devs):
            gath_copy(it, j, sub).wait_send()
        for j in range(1, groups):
            mid_copy(it, j, grp).wait_send()
        return carry

    lax.fori_loop(0, ITERS, drain, 0)


def per_device(
    right_side,
    noise_var,
    near_tiles,
    near_index,
    leaf_basis,
    leaf_transfer,
    leaf_coupling,
    far_leaf,
    dev_transfer,
    dev_coupling,
    far_dev,
    mid_coupling,
    far_mid,
):
    leaves, near, size, _ = near_tiles.shape
    probes = right_side.shape[1]
    rank = leaf_basis.shape[1]
    groups = lax.axis_size("grp")
    group_devs = lax.axis_size("sub")
    window = leaves + 2 * SPAN
    all_mids = groups * (group_devs // MID_DEVS)
    bf16, f32, i32 = jnp.bfloat16, jnp.float32, jnp.int32
    dma = pltpu.SemaphoreType.DMA
    operands = [
        near_index,
        far_leaf.T,
        far_dev,
        far_mid,
        right_side.reshape(leaves, size, probes),
        noise_var.reshape(-1, probes),
        leaf_basis,
        leaf_transfer,
        leaf_coupling,
        dev_transfer,
        dev_coupling,
        mid_coupling,
        near_tiles,
    ]
    scratch = [pltpu.SMEM(a.shape, i32) for a in operands[:4]]
    scratch += [pltpu.SMEM(a.shape, i32) for a in operands[:2]]
    scratch += [pltpu.VMEM(a.shape, a.dtype) for a in operands[4:]]
    scratch += [
        pltpu.VMEM((leaves, size, probes), f32),
        pltpu.VMEM((leaves, size, rank), bf16),
        pltpu.VMEM((leaves, rank, (far_leaf.shape[1] + 1) * rank), bf16),
        pltpu.VMEM((leaves, rank, probes), bf16),
        pltpu.VMEM((rank, rank), bf16),
        pltpu.VMEM((window, rank, probes), bf16),
        pltpu.VMEM((2 * SPAN, rank, size), bf16),
        pltpu.VMEM((group_devs, rank, rank), bf16),
        pltpu.VMEM((group_devs, rank, probes), bf16),
        pltpu.VMEM((all_mids, rank, probes), bf16),
        pltpu.VMEM((leaves, size, probes), f32),
        pltpu.VMEM((window, size, probes), bf16),
        pltpu.VMEM((ITERS + 1, leaves, size, probes), bf16),
        pltpu.VMEM((ITERS, 2 * SPAN, size, probes), bf16),
        pltpu.VMEM((ITERS, group_devs, rank, probes), bf16),
        pltpu.VMEM((ITERS, all_mids, rank, probes), bf16),
        dma((12,)),
        dma((leaves,)),
        dma((ITERS, 2, SPAN)),
        dma((ITERS, 2, SPAN)),
        dma((2,)),
        dma((2,)),
        dma((group_devs,)),
        dma((group_devs,)),
        dma((ITERS, group_devs)),
        dma((ITERS, group_devs)),
        dma((ITERS, groups)),
        dma((ITERS, groups)),
    ]
    result = pl.pallas_call(
        functools.partial(kernel, groups, group_devs),
        out_shape=jax.ShapeDtypeStruct((leaves, size, probes), f32),
        in_specs=[pl.BlockSpec(memory_space=pl.ANY)] * len(operands),
        out_specs=pl.BlockSpec(memory_space=pltpu.VMEM),
        scratch_shapes=scratch,
        compiler_params=pltpu.CompilerParams(
            collective_id=0, has_side_effects=True, vmem_limit_bytes=56 * 1024 * 1024
        ),
    )(*operands)
    return result.reshape(leaves * size, probes)


def solution(mesh):
    return jax.shard_map(
        per_device,
        mesh=mesh,
        in_specs=(
            P(("sub", "grp"), None),
            P(("sub", "grp")),
            P(("sub", "grp"), None, None, None),
            P(("sub", "grp"), None),
            P(("sub", "grp"), None, None),
            P(("sub", "grp"), None, None),
            P(("sub", "grp"), None, None, None),
            P(("sub", "grp"), None),
            P(("sub", "grp"), None, None),
            P(("sub", "grp"), None, None, None),
            P(("sub", "grp"), None),
            P("grp", None, None, None),
            P("grp", None),
        ),
        out_specs=P(("sub", "grp"), None),
        check_vma=False,
    )
```

```python
import functools

import jax
import jax.numpy as jnp
from jax import lax
from jax.experimental import pallas as pl
from jax.experimental.pallas import tpu as pltpu
from jax.sharding import PartitionSpec as P

SPAN = 6
ITERS = 4
MID_DEVS = 8
MESH = pl.DeviceIdType.MESH


relax_step = 0.3


def dot(a, b):
    return jnp.dot(a, b, preferred_element_type=jnp.float32)


def flip(a):
    return a.astype(jnp.float32).T.astype(jnp.bfloat16)


def kernel(
    groups,
    group_devs,
    near_hbm,
    far_hbm,
    fdev_hbm,
    fmid_hbm,
    rhs_hbm,
    noise_hbm,
    basis_hbm,
    lt_hbm,
    lc_hbm,
    dt_hbm,
    dc_hbm,
    mc_hbm,
    tiles_hbm,
    x_ref,
    near_raw,
    far_raw,
    fdev_ref,
    fmid_ref,
    near_ref,
    far_ref,
    rhs_ref,
    noise_raw,
    basis_ref,
    lt_ref,
    lc_ref,
    dt_ref,
    dc_ref,
    mc_ref,
    tiles,
    noise_ref,
    basis_t,
    far_all,
    field_ref,
    dt_t,
    cwin,
    nbasis,
    dt_all,
    gath_here,
    mid_here,
    image_ref,
    win,
    out,
    inc,
    gath,
    mid,
    in_sem,
    tile_sem,
    halo_send,
    halo_recv,
    nb_send,
    nb_recv,
    dt_send,
    dt_recv,
    g_send,
    g_recv,
    m_send,
    m_recv,
):
    leaves, size, probes = rhs_ref.shape
    rank = basis_ref.shape[1]
    near = near_ref.shape[1]
    nfar = far_ref.shape[0]
    nfdev = fdev_ref.shape[1]
    nfmid = fmid_ref.shape[1]
    mid_grp = group_devs // MID_DEVS
    count = groups * group_devs
    sub = lax.axis_index("sub")
    grp = lax.axis_index("grp")
    me = sub * groups + grp
    nxt = lax.rem(me + 1, count)
    prv = lax.rem(me + count - 1, count)
    next_id = (nxt // groups, lax.rem(nxt, groups))
    prev_id = (prv // groups, lax.rem(prv, groups))

    operands = [
        (rhs_hbm, rhs_ref),
        (basis_hbm, basis_ref),
        (dt_hbm, dt_ref),
        (lt_hbm, lt_ref),
        (near_hbm, near_raw),
        (far_hbm, far_raw),
        (fdev_hbm, fdev_ref),
        (fmid_hbm, fmid_ref),
        (noise_hbm, noise_raw),
        (lc_hbm, lc_ref),
        (dc_hbm, dc_ref),
        (mc_hbm, mc_ref),
    ]
    loads = [
        pltpu.make_async_copy(src, dst, in_sem.at[i]) for i, (src, dst) in enumerate(operands)
    ]
    for load in loads:
        load.start()
    tile_loads = [
        pltpu.make_async_copy(tiles_hbm.at[l], tiles.at[l], tile_sem.at[l]) for l in range(leaves)
    ]
    for load in tile_loads:
        load.start()

    def sub_peer(j):
        return lax.rem(sub + j, group_devs)

    def grp_peer(j):
        return lax.rem(grp + j, groups)

    def remote(src, dst, send, recv, device):
        return pltpu.make_async_remote_copy(
            src_ref=src,
            dst_ref=dst,
            send_sem=send,
            recv_sem=recv,
            device_id=device,
            device_id_type=MESH,
        )

    def to_prev(it, h):
        return remote(
            out.at[it, h],
            inc.at[it, SPAN + h],
            halo_send.at[it, 0, h],
            halo_recv.at[it, 0, h],
            prev_id,
        )

    def to_next(it, h):
        return remote(
            out.at[it, leaves - SPAN + h],
            inc.at[it, h],
            halo_send.at[it, 1, h],
            halo_recv.at[it, 1, h],
            next_id,
        )

    def basis_copy(side):
        if side == 0:
            src, dst, device = basis_ref.at[pl.ds(0, SPAN)], nbasis.at[pl.ds(SPAN, SPAN)], prev_id
        else:
            src, dst, device = (
                basis_ref.at[pl.ds(leaves - SPAN, SPAN)],
                nbasis.at[pl.ds(0, SPAN)],
                next_id,
            )
        return remote(src, dst, nb_send.at[side], nb_recv.at[side], device)

    def dt_copy(j, owner):
        return remote(
            dt_ref.at[0], dt_all.at[owner], dt_send.at[j], dt_recv.at[j], (sub_peer(j), grp)
        )

    def gath_copy(it, j, owner):
        block = gath.at[it, owner]
        return remote(block, block, g_send.at[it, j], g_recv.at[it, j], (sub_peer(j), grp))

    def mid_copy(it, j, owner):
        block = mid.at[it, pl.ds(owner * mid_grp, mid_grp)]
        return remote(block, block, m_send.at[it, j], m_recv.at[it, j], (sub, grp_peer(j)))

    early = SPAN // 2
    middle = early + 1
    prev_order = list(range(SPAN))
    next_order = list(range(SPAN - 1, -1, -1))
    first = prev_order[:early]
    last = [leaves - SPAN + h for h in next_order[:early]]

    def steps_needed(l):
        return min(SPAN, max(0, SPAN - l, l + SPAN - leaves + 1))

    by_step = [[l for l in range(leaves) if steps_needed(l) == n] for n in range(SPAN + 1)]

    def sends_first(batch):
        return sorted(batch, key=lambda l: (l not in first and l not in last, l))

    def stage(it, steps):
        for step in steps:
            to_next(it, next_order[step]).wait_recv()
            to_prev(it, prev_order[step]).wait_recv()
        for step in steps:
            for h in (next_order[step], SPAN + prev_order[step]):
                place = h if h < SPAN else leaves + h
                block = inc[it, h]
                win[place] = block
                cwin[place] = dot(nbasis[h], block).astype(jnp.bfloat16)

    def near_part(l):
        image = dot(tiles[l, 0], win[near_ref[l, 0]])
        for k in range(1, near):
            image = image + dot(tiles[l, k], win[near_ref[l, k]])
        return image

    barrier = pltpu.get_barrier_semaphore()
    for device in (prev_id, next_id):
        pl.semaphore_signal(barrier, inc=1, device_id=device, device_id_type=MESH)
    for j in range(1, group_devs):
        pl.semaphore_signal(barrier, inc=1, device_id=(sub_peer(j), grp), device_id_type=MESH)
    for j in range(1, groups):
        pl.semaphore_signal(barrier, inc=1, device_id=(sub, grp_peer(j)), device_id_type=MESH)

    loads[0].wait()
    for l in range(leaves):
        start = relax_step * rhs_ref[l]
        x_ref[l] = start
        out[0, l] = start.astype(jnp.bfloat16)
    pl.semaphore_wait(barrier, 2 + (group_devs - 1) + (groups - 1))

    for step in range(early):
        to_prev(0, prev_order[step]).start()
        to_next(0, next_order[step]).start()
    for load in loads[1:]:
        load.wait()
    for j in range(1, group_devs):
        dt_copy(j, sub).start()
    basis_copy(0).start()
    basis_copy(1).start()

    total_leaves = leaves * count
    window = leaves + 2 * SPAN
    for l in range(leaves):
        for k in range(near):
            place = near_raw[l, k] - me * leaves + SPAN
            place = jnp.where(place < 0, place + total_leaves, place)
            place = jnp.where(place >= total_leaves, place - total_leaves, place)
            near_ref[l, k] = jnp.minimum(place, window - 1)
        for k in range(nfar):
            place = far_raw[k, l] - me * leaves + SPAN
            place = jnp.where(place < 0, place + total_leaves, place)
            place = jnp.where(place >= total_leaves, place - total_leaves, place)
            far_ref[k, l] = jnp.minimum(place, window - 1)

    dt_all[sub] = dt_ref[0]
    dt_t[...] = flip(dt_ref[0])
    lanes = noise_raw.shape[1]
    pieces = size // lanes
    for l in range(leaves):
        basis_t[l] = flip(basis_ref[l])
        for k in range(nfar):
            far_all[l, :, pl.ds(k * rank, rank)] = lc_ref[l, k]
        far_all[l, :, pl.ds(nfar * rank, rank)] = flip(lt_ref[l])
        for c in range(pieces):
            row = noise_raw[pl.ds(l * pieces + c, 1), :]
            noise_ref[l, pl.ds(c * lanes, lanes), :] = jnp.broadcast_to(row, (probes, lanes)).T
    for j in range(1, group_devs):
        dt_copy(j, lax.rem(sub + group_devs - j, group_devs)).wait_recv()
    for load in tile_loads:
        load.wait()

    def sweep(it, carry):
        total = None
        for l in range(leaves):
            block = out[it, l]
            win[SPAN + l] = block
            coef = dot(basis_ref[l], block).astype(jnp.bfloat16)
            cwin[SPAN + l] = coef
            term = dot(lt_ref[l], coef)
            total = term if total is None else total + term
        gath[it, sub] = total.astype(jnp.bfloat16)
        for j in range(1, group_devs):
            gath_copy(it, j, sub).start()
        for step in range(early, middle):
            to_prev(it, prev_order[step]).start()
            to_next(it, next_order[step]).start()

        @pl.when(it == 0)
        def _():
            basis_copy(0).wait_recv()
            basis_copy(1).wait_recv()

        def arrive(steps):
            stage(it, steps)
            for step in steps:
                for l in by_step[step + 1]:
                    image_ref[l] = near_part(l)

        for l in by_step[0]:
            image_ref[l] = near_part(l)
        arrive(range(early))

        for j in range(1, group_devs):
            gath_copy(it, j, lax.rem(sub + group_devs - j, group_devs)).wait_recv()
        for m in range(mid_grp):
            lifted = None
            for s in range(MID_DEVS):
                place = m * MID_DEVS + s
                coef = gath[it, place]
                gath_here[place] = coef
                term = dot(dt_all[place], coef).astype(jnp.bfloat16).astype(jnp.float32)
                lifted = term if lifted is None else lifted + term
            mid[it, grp * mid_grp + m] = lifted.astype(jnp.bfloat16)
        for j in range(1, groups):
            mid_copy(it, j, grp).start()
        for step in range(middle, SPAN):
            to_prev(it, prev_order[step]).start()
            to_next(it, next_order[step]).start()

        dev_total = None
        for k in range(nfdev):
            term = dot(dc_ref[0, k], gath_here[lax.div(fdev_ref[0, k], groups)])
            dev_total = term if dev_total is None else dev_total + term

        arrive(range(early, middle))

        for j in range(1, groups):
            mid_copy(it, j, lax.rem(grp + groups - j, groups)).wait_recv()
        for m in range(groups * mid_grp):
            mid_here[m] = mid[it, m]
        own_mid = sub // MID_DEVS
        field = None
        for k in range(nfmid):
            term = dot(mc_ref[own_mid, k], mid_here[fmid_ref[own_mid, k]])
            field = term if field is None else field + term
        dev_field = (dev_total + dot(dt_t[...], field.astype(jnp.bfloat16))).astype(jnp.bfloat16)

        def finish(batch):
            for l in batch:
                parts = [cwin[far_ref[k, l]] for k in range(nfar)] + [dev_field]
                field_ref[l] = dot(far_all[l], jnp.concatenate(parts, axis=0)).astype(jnp.bfloat16)
            for at in range(0, len(batch), 2):
                pair = batch[at : at + 2]
                for l in pair:
                    image = image_ref[l] + dot(basis_t[l], field_ref[l])
                    old = x_ref[l]
                    image = image + noise_ref[l] * old
                    new = old + relax_step * (rhs_ref[l] - image)
                    x_ref[l] = new
                    out[it + 1, l] = new.astype(jnp.bfloat16)
                if any(l in first or l in last for l in pair):

                    @pl.when(it + 1 < ITERS)
                    def _():
                        for l in pair:
                            if l in first:
                                to_prev(it + 1, l).start()
                            if l in last:
                                to_next(it + 1, l - (leaves - SPAN)).start()

        done = [l for step in range(middle + 1) for l in reversed(by_step[step])]
        finish(sends_first(done))

        @pl.when(it == 0)
        def _():
            for j in range(1, group_devs):
                dt_copy(j, sub).wait_send()
            basis_copy(0).wait_send()
            basis_copy(1).wait_send()

        for j in range(1, group_devs):
            gath_copy(it, j, sub).wait_send()
        for j in range(1, groups):
            mid_copy(it, j, grp).wait_send()
        for h in range(SPAN):
            to_prev(it, h).wait_send()
            to_next(it, h).wait_send()
        arrive(range(middle, SPAN))
        finish(sends_first([l for l in range(leaves) if l not in done]))
        return carry

    lax.fori_loop(0, ITERS, sweep, 0)


def per_device(
    right_side,
    noise_var,
    near_tiles,
    near_index,
    leaf_basis,
    leaf_transfer,
    leaf_coupling,
    far_leaf,
    dev_transfer,
    dev_coupling,
    far_dev,
    mid_coupling,
    far_mid,
):
    leaves, near, size, _ = near_tiles.shape
    probes = right_side.shape[1]
    rank = leaf_basis.shape[1]
    groups = lax.axis_size("grp")
    group_devs = lax.axis_size("sub")
    window = leaves + 2 * SPAN
    all_mids = groups * (group_devs // MID_DEVS)
    bf16, f32, i32 = jnp.bfloat16, jnp.float32, jnp.int32
    dma = pltpu.SemaphoreType.DMA
    operands = [
        near_index,
        far_leaf.T,
        far_dev,
        far_mid,
        right_side.reshape(leaves, size, probes),
        noise_var.reshape(-1, probes),
        leaf_basis,
        leaf_transfer,
        leaf_coupling,
        dev_transfer,
        dev_coupling,
        mid_coupling,
        near_tiles,
    ]
    scratch = [pltpu.SMEM(a.shape, i32) for a in operands[:4]]
    scratch += [pltpu.SMEM(a.shape, i32) for a in operands[:2]]
    scratch += [pltpu.VMEM(a.shape, a.dtype) for a in operands[4:]]
    scratch += [
        pltpu.VMEM((leaves, size, probes), f32),
        pltpu.VMEM((leaves, size, rank), bf16),
        pltpu.VMEM((leaves, rank, (far_leaf.shape[1] + 1) * rank), bf16),
        pltpu.VMEM((leaves, rank, probes), bf16),
        pltpu.VMEM((rank, rank), bf16),
        pltpu.VMEM((window, rank, probes), bf16),
        pltpu.VMEM((2 * SPAN, rank, size), bf16),
        pltpu.VMEM((group_devs, rank, rank), bf16),
        pltpu.VMEM((group_devs, rank, probes), bf16),
        pltpu.VMEM((all_mids, rank, probes), bf16),
        pltpu.VMEM((leaves, size, probes), f32),
        pltpu.VMEM((window, size, probes), bf16),
        pltpu.VMEM((ITERS + 1, leaves, size, probes), bf16),
        pltpu.VMEM((ITERS, 2 * SPAN, size, probes), bf16),
        pltpu.VMEM((ITERS, group_devs, rank, probes), bf16),
        pltpu.VMEM((ITERS, all_mids, rank, probes), bf16),
        dma((12,)),
        dma((leaves,)),
        dma((ITERS, 2, SPAN)),
        dma((ITERS, 2, SPAN)),
        dma((2,)),
        dma((2,)),
        dma((group_devs,)),
        dma((group_devs,)),
        dma((ITERS, group_devs)),
        dma((ITERS, group_devs)),
        dma((ITERS, groups)),
        dma((ITERS, groups)),
    ]
    result = pl.pallas_call(
        functools.partial(kernel, groups, group_devs),
        out_shape=jax.ShapeDtypeStruct((leaves, size, probes), f32),
        in_specs=[pl.BlockSpec(memory_space=pl.ANY)] * len(operands),
        out_specs=pl.BlockSpec(memory_space=pltpu.VMEM),
        scratch_shapes=scratch,
        compiler_params=pltpu.CompilerParams(
            collective_id=0, has_side_effects=True, vmem_limit_bytes=56 * 1024 * 1024
        ),
    )(*operands)
    return result.reshape(leaves * size, probes)


def solution(mesh):
    return jax.shard_map(
        per_device,
        mesh=mesh,
        in_specs=(
            P(("sub", "grp"), None),
            P(("sub", "grp")),
            P(("sub", "grp"), None, None, None),
            P(("sub", "grp"), None),
            P(("sub", "grp"), None, None),
            P(("sub", "grp"), None, None),
            P(("sub", "grp"), None, None, None),
            P(("sub", "grp"), None),
            P(("sub", "grp"), None, None),
            P(("sub", "grp"), None, None, None),
            P(("sub", "grp"), None),
            P("grp", None, None, None),
            P("grp", None),
        ),
        out_specs=P(("sub", "grp"), None),
        check_vma=False,
    )
```

```python
import functools

import jax
import jax.numpy as jnp
from jax import lax
from jax.experimental import pallas as pl
from jax.experimental.pallas import tpu as pltpu
from jax.sharding import PartitionSpec as P

SPAN = 6
ITERS = 4
MID_DEVS = 8
MESH = pl.DeviceIdType.MESH


relax_step = 0.3


def dot(a, b):
    return jnp.dot(a, b, preferred_element_type=jnp.float32)


def flip(a):
    return a.astype(jnp.float32).T.astype(jnp.bfloat16)


def kernel(
    groups,
    group_devs,
    near_hbm,
    far_hbm,
    fdev_hbm,
    fmid_hbm,
    rhs_hbm,
    noise_hbm,
    basis_hbm,
    lt_hbm,
    lc_hbm,
    dt_hbm,
    dc_hbm,
    mc_hbm,
    tiles_hbm,
    x_ref,
    near_raw,
    far_raw,
    fdev_ref,
    fmid_ref,
    near_ref,
    far_ref,
    rhs_ref,
    noise_raw,
    basis_ref,
    lt_ref,
    lc_ref,
    dt_ref,
    dc_ref,
    mc_ref,
    tiles,
    noise_ref,
    basis_t,
    far_all,
    field_ref,
    dt_t,
    cwin,
    nbasis,
    dt_all,
    gath_here,
    mid_here,
    image_ref,
    win,
    out,
    inc,
    gath,
    mid,
    in_sem,
    tile_sem,
    halo_send,
    halo_recv,
    nb_send,
    nb_recv,
    dt_send,
    dt_recv,
    g_send,
    g_recv,
    m_send,
    m_recv,
):
    leaves, size, probes = rhs_ref.shape
    rank = basis_ref.shape[1]
    near = near_ref.shape[1]
    nfar = far_ref.shape[0]
    nfdev = fdev_ref.shape[1]
    nfmid = fmid_ref.shape[1]
    mid_grp = group_devs // MID_DEVS
    count = groups * group_devs
    sub = lax.axis_index("sub")
    grp = lax.axis_index("grp")
    me = sub * groups + grp
    nxt = lax.rem(me + 1, count)
    prv = lax.rem(me + count - 1, count)
    next_id = (nxt // groups, lax.rem(nxt, groups))
    prev_id = (prv // groups, lax.rem(prv, groups))

    operands = [
        (rhs_hbm, rhs_ref),
        (basis_hbm, basis_ref),
        (dt_hbm, dt_ref),
        (lt_hbm, lt_ref),
        (near_hbm, near_raw),
        (far_hbm, far_raw),
        (fdev_hbm, fdev_ref),
        (fmid_hbm, fmid_ref),
        (noise_hbm, noise_raw),
        (lc_hbm, lc_ref),
        (dc_hbm, dc_ref),
        (mc_hbm, mc_ref),
    ]
    loads = [
        pltpu.make_async_copy(src, dst, in_sem.at[i]) for i, (src, dst) in enumerate(operands)
    ]
    for load in loads:
        load.start()
    tile_loads = [
        pltpu.make_async_copy(
            tiles_hbm.at[l, k], tiles.at[l, :, pl.ds(k * size, size)], tile_sem.at[l, k]
        )
        for l in range(leaves)
        for k in range(near)
    ]
    for load in tile_loads:
        load.start()

    def sub_peer(j):
        return lax.rem(sub + j, group_devs)

    def grp_peer(j):
        return lax.rem(grp + j, groups)

    def remote(src, dst, send, recv, device):
        return pltpu.make_async_remote_copy(
            src_ref=src,
            dst_ref=dst,
            send_sem=send,
            recv_sem=recv,
            device_id=device,
            device_id_type=MESH,
        )

    def to_prev(it, h):
        return remote(
            out.at[it, h],
            inc.at[it, SPAN + h],
            halo_send.at[it, 0, h],
            halo_recv.at[it, 0, h],
            prev_id,
        )

    def to_next(it, h):
        return remote(
            out.at[it, leaves - SPAN + h],
            inc.at[it, h],
            halo_send.at[it, 1, h],
            halo_recv.at[it, 1, h],
            next_id,
        )

    def basis_copy(side):
        if side == 0:
            src, dst, device = basis_ref.at[pl.ds(0, SPAN)], nbasis.at[pl.ds(SPAN, SPAN)], prev_id
        else:
            src, dst, device = (
                basis_ref.at[pl.ds(leaves - SPAN, SPAN)],
                nbasis.at[pl.ds(0, SPAN)],
                next_id,
            )
        return remote(src, dst, nb_send.at[side], nb_recv.at[side], device)

    def dt_copy(j, owner):
        return remote(
            dt_ref.at[0], dt_all.at[owner], dt_send.at[j], dt_recv.at[j], (sub_peer(j), grp)
        )

    def gath_copy(it, j, owner):
        block = gath.at[it, owner]
        return remote(block, block, g_send.at[it, j], g_recv.at[it, j], (sub_peer(j), grp))

    def mid_copy(it, j, owner):
        block = mid.at[it, pl.ds(owner * mid_grp, mid_grp)]
        return remote(block, block, m_send.at[it, j], m_recv.at[it, j], (sub, grp_peer(j)))

    early = SPAN // 2
    middle = SPAN - 1
    prev_order = list(range(SPAN))
    next_order = list(range(SPAN - 1, -1, -1))
    first = prev_order[:early]
    last = [leaves - SPAN + h for h in next_order[:early]]

    def steps_needed(l):
        return min(SPAN, max(0, SPAN - l, l + SPAN - leaves + 1))

    by_step = [[l for l in range(leaves) if steps_needed(l) == n] for n in range(SPAN + 1)]

    def sends_first(batch):
        return sorted(batch, key=lambda l: (l not in first and l not in last, l))

    def stage(it, steps):
        for step in steps:
            to_next(it, next_order[step]).wait_recv()
            to_prev(it, prev_order[step]).wait_recv()
        for step in steps:
            for h in (next_order[step], SPAN + prev_order[step]):
                place = h if h < SPAN else leaves + h
                block = inc[it, h]
                win[place] = block
                cwin[place] = dot(nbasis[h], block).astype(jnp.bfloat16)

    def near_part(l):
        image = dot(tiles[l], jnp.concatenate([win[near_ref[l, k]] for k in range(near)], axis=0))
        return image

    barrier = pltpu.get_barrier_semaphore()
    for device in (prev_id, next_id):
        pl.semaphore_signal(barrier, inc=1, device_id=device, device_id_type=MESH)
    for j in range(1, group_devs):
        pl.semaphore_signal(barrier, inc=1, device_id=(sub_peer(j), grp), device_id_type=MESH)
    for j in range(1, groups):
        pl.semaphore_signal(barrier, inc=1, device_id=(sub, grp_peer(j)), device_id_type=MESH)

    loads[0].wait()
    for l in range(leaves):
        start = relax_step * rhs_ref[l]
        x_ref[l] = start
        out[0, l] = start.astype(jnp.bfloat16)
    pl.semaphore_wait(barrier, 2 + (group_devs - 1) + (groups - 1))

    for step in range(early):
        to_prev(0, prev_order[step]).start()
        to_next(0, next_order[step]).start()
    for load in loads[1:]:
        load.wait()
    for j in range(1, group_devs):
        dt_copy(j, sub).start()
    basis_copy(0).start()
    basis_copy(1).start()

    total_leaves = leaves * count
    window = leaves + 2 * SPAN
    for l in range(leaves):
        for k in range(near):
            place = near_raw[l, k] - me * leaves + SPAN
            place = jnp.where(place < 0, place + total_leaves, place)
            place = jnp.where(place >= total_leaves, place - total_leaves, place)
            near_ref[l, k] = jnp.minimum(place, window - 1)
        for k in range(nfar):
            place = far_raw[k, l] - me * leaves + SPAN
            place = jnp.where(place < 0, place + total_leaves, place)
            place = jnp.where(place >= total_leaves, place - total_leaves, place)
            far_ref[k, l] = jnp.minimum(place, window - 1)

    dt_all[sub] = dt_ref[0]
    dt_t[...] = flip(dt_ref[0])
    lanes = noise_raw.shape[1]
    pieces = size // lanes
    for l in range(leaves):
        basis_t[l] = flip(basis_ref[l])
        for k in range(nfar):
            far_all[l, :, pl.ds(k * rank, rank)] = lc_ref[l, k]
        far_all[l, :, pl.ds(nfar * rank, rank)] = flip(lt_ref[l])
        for c in range(pieces):
            row = noise_raw[pl.ds(l * pieces + c, 1), :]
            noise_ref[l, pl.ds(c * lanes, lanes), :] = jnp.broadcast_to(row, (probes, lanes)).T
    for j in range(1, group_devs):
        dt_copy(j, lax.rem(sub + group_devs - j, group_devs)).wait_recv()
    for load in tile_loads:
        load.wait()

    def sweep(it, carry):
        total = None
        for l in range(leaves):
            block = out[it, l]
            win[SPAN + l] = block
            coef = dot(basis_ref[l], block).astype(jnp.bfloat16)
            cwin[SPAN + l] = coef
            term = dot(lt_ref[l], coef)
            total = term if total is None else total + term
        gath[it, sub] = total.astype(jnp.bfloat16)
        for j in range(1, group_devs):
            gath_copy(it, j, sub).start()
        for step in range(early, middle):
            to_prev(it, prev_order[step]).start()
            to_next(it, next_order[step]).start()

        @pl.when(it == 0)
        def _():
            basis_copy(0).wait_recv()
            basis_copy(1).wait_recv()

        def arrive(steps):
            stage(it, steps)
            for step in steps:
                for l in by_step[step + 1]:
                    image_ref[l] = near_part(l)

        for l in by_step[0]:
            image_ref[l] = near_part(l)
        arrive(range(early))

        for j in range(1, group_devs):
            gath_copy(it, j, lax.rem(sub + group_devs - j, group_devs)).wait_recv()
        for m in range(mid_grp):
            lifted = None
            for s in range(MID_DEVS):
                place = m * MID_DEVS + s
                coef = gath[it, place]
                gath_here[place] = coef
                term = dot(dt_all[place], coef).astype(jnp.bfloat16).astype(jnp.float32)
                lifted = term if lifted is None else lifted + term
            mid[it, grp * mid_grp + m] = lifted.astype(jnp.bfloat16)
        for j in range(1, groups):
            mid_copy(it, j, grp).start()
        for step in range(middle, SPAN):
            to_prev(it, prev_order[step]).start()
            to_next(it, next_order[step]).start()

        dev_total = None
        for k in range(nfdev):
            term = dot(dc_ref[0, k], gath_here[lax.div(fdev_ref[0, k], groups)])
            dev_total = term if dev_total is None else dev_total + term

        arrive(range(early, middle))

        for j in range(1, groups):
            mid_copy(it, j, lax.rem(grp + groups - j, groups)).wait_recv()
        for m in range(groups * mid_grp):
            mid_here[m] = mid[it, m]
        own_mid = sub // MID_DEVS
        field = None
        for k in range(nfmid):
            term = dot(mc_ref[own_mid, k], mid_here[fmid_ref[own_mid, k]])
            field = term if field is None else field + term
        dev_field = (dev_total + dot(dt_t[...], field.astype(jnp.bfloat16))).astype(jnp.bfloat16)

        def finish(batch):
            for l in batch:
                parts = [cwin[far_ref[k, l]] for k in range(nfar)] + [dev_field]
                field_ref[l] = dot(far_all[l], jnp.concatenate(parts, axis=0)).astype(jnp.bfloat16)
            for at in range(0, len(batch), 2):
                pair = batch[at : at + 2]
                for l in pair:
                    image = image_ref[l] + dot(basis_t[l], field_ref[l])
                    old = x_ref[l]
                    image = image + noise_ref[l] * old
                    new = old + relax_step * (rhs_ref[l] - image)
                    x_ref[l] = new
                    out[it + 1, l] = new.astype(jnp.bfloat16)
                if any(l in first or l in last for l in pair):

                    @pl.when(it + 1 < ITERS)
                    def _():
                        for l in pair:
                            if l in first:
                                to_prev(it + 1, l).start()
                            if l in last:
                                to_next(it + 1, l - (leaves - SPAN)).start()

        done = [l for step in range(middle + 1) for l in reversed(by_step[step])]
        finish(sends_first(done))

        @pl.when(it == 0)
        def _():
            for j in range(1, group_devs):
                dt_copy(j, sub).wait_send()
            basis_copy(0).wait_send()
            basis_copy(1).wait_send()

        for j in range(1, group_devs):
            gath_copy(it, j, sub).wait_send()
        for j in range(1, groups):
            mid_copy(it, j, grp).wait_send()
        for h in range(SPAN):
            to_prev(it, h).wait_send()
            to_next(it, h).wait_send()
        arrive(range(middle, SPAN))
        finish(sends_first([l for l in range(leaves) if l not in done]))
        return carry

    lax.fori_loop(0, ITERS, sweep, 0)


def per_device(
    right_side,
    noise_var,
    near_tiles,
    near_index,
    leaf_basis,
    leaf_transfer,
    leaf_coupling,
    far_leaf,
    dev_transfer,
    dev_coupling,
    far_dev,
    mid_coupling,
    far_mid,
):
    leaves, near, size, _ = near_tiles.shape
    probes = right_side.shape[1]
    rank = leaf_basis.shape[1]
    groups = lax.axis_size("grp")
    group_devs = lax.axis_size("sub")
    window = leaves + 2 * SPAN
    all_mids = groups * (group_devs // MID_DEVS)
    bf16, f32, i32 = jnp.bfloat16, jnp.float32, jnp.int32
    dma = pltpu.SemaphoreType.DMA
    operands = [
        near_index,
        far_leaf.T,
        far_dev,
        far_mid,
        right_side.reshape(leaves, size, probes),
        noise_var.reshape(-1, probes),
        leaf_basis,
        leaf_transfer,
        leaf_coupling,
        dev_transfer,
        dev_coupling,
        mid_coupling,
        near_tiles,
    ]
    scratch = [pltpu.SMEM(a.shape, i32) for a in operands[:4]]
    scratch += [pltpu.SMEM(a.shape, i32) for a in operands[:2]]
    scratch += [pltpu.VMEM(a.shape, a.dtype) for a in operands[4:-1]]
    scratch += [pltpu.VMEM((leaves, size, near * size), bf16)]
    scratch += [
        pltpu.VMEM((leaves, size, probes), f32),
        pltpu.VMEM((leaves, size, rank), bf16),
        pltpu.VMEM((leaves, rank, (far_leaf.shape[1] + 1) * rank), bf16),
        pltpu.VMEM((leaves, rank, probes), bf16),
        pltpu.VMEM((rank, rank), bf16),
        pltpu.VMEM((window, rank, probes), bf16),
        pltpu.VMEM((2 * SPAN, rank, size), bf16),
        pltpu.VMEM((group_devs, rank, rank), bf16),
        pltpu.VMEM((group_devs, rank, probes), bf16),
        pltpu.VMEM((all_mids, rank, probes), bf16),
        pltpu.VMEM((leaves, size, probes), f32),
        pltpu.VMEM((window, size, probes), bf16),
        pltpu.VMEM((ITERS + 1, leaves, size, probes), bf16),
        pltpu.VMEM((ITERS, 2 * SPAN, size, probes), bf16),
        pltpu.VMEM((ITERS, group_devs, rank, probes), bf16),
        pltpu.VMEM((ITERS, all_mids, rank, probes), bf16),
        dma((12,)),
        dma((leaves, near)),
        dma((ITERS, 2, SPAN)),
        dma((ITERS, 2, SPAN)),
        dma((2,)),
        dma((2,)),
        dma((group_devs,)),
        dma((group_devs,)),
        dma((ITERS, group_devs)),
        dma((ITERS, group_devs)),
        dma((ITERS, groups)),
        dma((ITERS, groups)),
    ]
    result = pl.pallas_call(
        functools.partial(kernel, groups, group_devs),
        out_shape=jax.ShapeDtypeStruct((leaves, size, probes), f32),
        in_specs=[pl.BlockSpec(memory_space=pl.ANY)] * len(operands),
        out_specs=pl.BlockSpec(memory_space=pltpu.VMEM),
        scratch_shapes=scratch,
        compiler_params=pltpu.CompilerParams(
            collective_id=0, has_side_effects=True, vmem_limit_bytes=56 * 1024 * 1024
        ),
    )(*operands)
    return result.reshape(leaves * size, probes)


def solution(mesh):
    return jax.shard_map(
        per_device,
        mesh=mesh,
        in_specs=(
            P(("sub", "grp"), None),
            P(("sub", "grp")),
            P(("sub", "grp"), None, None, None),
            P(("sub", "grp"), None),
            P(("sub", "grp"), None, None),
            P(("sub", "grp"), None, None),
            P(("sub", "grp"), None, None, None),
            P(("sub", "grp"), None),
            P(("sub", "grp"), None, None),
            P(("sub", "grp"), None, None, None),
            P(("sub", "grp"), None),
            P("grp", None, None, None),
            P("grp", None),
        ),
        out_specs=P(("sub", "grp"), None),
        check_vma=False,
    )
```

```python
import functools

import jax
import jax.numpy as jnp
from jax import lax
from jax.experimental import pallas as pl
from jax.experimental.pallas import tpu as pltpu
from jax.sharding import PartitionSpec as P

SPAN = 6
ITERS = 4
MID_DEVS = 8
MESH = pl.DeviceIdType.MESH


relax_step = 0.3


def dot(a, b):
    return jnp.dot(a, b, preferred_element_type=jnp.float32)


def flip(a):
    return a.astype(jnp.float32).T.astype(jnp.bfloat16)


def kernel(
    groups,
    group_devs,
    near_hbm,
    far_hbm,
    fdev_hbm,
    fmid_hbm,
    rhs_hbm,
    noise_hbm,
    basis_hbm,
    lt_hbm,
    lc_hbm,
    dt_hbm,
    dc_hbm,
    mc_hbm,
    tiles_hbm,
    x_ref,
    near_raw,
    far_raw,
    fdev_ref,
    fmid_ref,
    near_ref,
    far_ref,
    rhs_ref,
    noise_raw,
    basis_ref,
    lt_ref,
    lc_ref,
    dt_ref,
    dc_ref,
    mc_ref,
    tiles,
    noise_ref,
    basis_t,
    far_all,
    field_ref,
    dt_t,
    cwin,
    nbasis,
    dt_all,
    gath_here,
    mid_here,
    image_ref,
    win,
    out,
    inc,
    gath,
    mid,
    in_sem,
    tile_sem,
    halo_send,
    halo_recv,
    nb_send,
    nb_recv,
    dt_send,
    dt_recv,
    g_send,
    g_recv,
    m_send,
    m_recv,
):
    leaves, size, probes = rhs_ref.shape
    rank = basis_ref.shape[1]
    near = near_ref.shape[1]
    nfar = far_ref.shape[0]
    nfdev = fdev_ref.shape[1]
    nfmid = fmid_ref.shape[1]
    mid_grp = group_devs // MID_DEVS
    count = groups * group_devs
    sub = lax.axis_index("sub")
    grp = lax.axis_index("grp")
    me = sub * groups + grp
    nxt = lax.rem(me + 1, count)
    prv = lax.rem(me + count - 1, count)
    next_id = (nxt // groups, lax.rem(nxt, groups))
    prev_id = (prv // groups, lax.rem(prv, groups))

    operands = [
        (rhs_hbm, rhs_ref),
        (basis_hbm, basis_ref),
        (dt_hbm, dt_ref),
        (lt_hbm, lt_ref),
        (near_hbm, near_raw),
        (far_hbm, far_raw),
        (fdev_hbm, fdev_ref),
        (fmid_hbm, fmid_ref),
        (noise_hbm, noise_raw),
        (lc_hbm, lc_ref),
        (dc_hbm, dc_ref),
        (mc_hbm, mc_ref),
    ]
    loads = [
        pltpu.make_async_copy(src, dst, in_sem.at[i]) for i, (src, dst) in enumerate(operands)
    ]
    for load in loads:
        load.start()
    tile_loads = [
        pltpu.make_async_copy(
            tiles_hbm.at[l, k], tiles.at[l, :, pl.ds(k * size, size)], tile_sem.at[l, k]
        )
        for l in range(leaves)
        for k in range(near)
    ]
    for load in tile_loads:
        load.start()

    def sub_peer(j):
        return lax.rem(sub + j, group_devs)

    def grp_peer(j):
        return lax.rem(grp + j, groups)

    def remote(src, dst, send, recv, device):
        return pltpu.make_async_remote_copy(
            src_ref=src,
            dst_ref=dst,
            send_sem=send,
            recv_sem=recv,
            device_id=device,
            device_id_type=MESH,
        )

    def to_prev(it, h):
        return remote(
            out.at[it, h],
            inc.at[it, SPAN + h],
            halo_send.at[it, 0, h],
            halo_recv.at[it, 0, h],
            prev_id,
        )

    def to_next(it, h):
        return remote(
            out.at[it, leaves - SPAN + h],
            inc.at[it, h],
            halo_send.at[it, 1, h],
            halo_recv.at[it, 1, h],
            next_id,
        )

    def basis_copy(side):
        if side == 0:
            src, dst, device = basis_ref.at[pl.ds(0, SPAN)], nbasis.at[pl.ds(SPAN, SPAN)], prev_id
        else:
            src, dst, device = (
                basis_ref.at[pl.ds(leaves - SPAN, SPAN)],
                nbasis.at[pl.ds(0, SPAN)],
                next_id,
            )
        return remote(src, dst, nb_send.at[side], nb_recv.at[side], device)

    def dt_copy(j, owner):
        return remote(
            dt_ref.at[0], dt_all.at[owner], dt_send.at[j], dt_recv.at[j], (sub_peer(j), grp)
        )

    def gath_copy(it, j, owner):
        block = gath.at[it, owner]
        return remote(block, block, g_send.at[it, j], g_recv.at[it, j], (sub_peer(j), grp))

    def mid_copy(it, j, owner):
        block = mid.at[it, pl.ds(owner * mid_grp, mid_grp)]
        return remote(block, block, m_send.at[it, j], m_recv.at[it, j], (sub, grp_peer(j)))

    early = SPAN // 2
    middle = SPAN - 1
    prev_order = list(range(SPAN))
    next_order = list(range(SPAN - 1, -1, -1))
    first = prev_order[:early]
    last = [leaves - SPAN + h for h in next_order[:early]]

    def steps_needed(l):
        return min(SPAN, max(0, SPAN - l, l + SPAN - leaves + 1))

    by_step = [[l for l in range(leaves) if steps_needed(l) == n] for n in range(SPAN + 1)]

    def sends_first(batch):
        return sorted(batch, key=lambda l: (l not in first and l not in last, l))

    def stage(it, steps):
        for step in steps:
            to_next(it, next_order[step]).wait_recv()
            to_prev(it, prev_order[step]).wait_recv()
        for step in steps:
            for h in (next_order[step], SPAN + prev_order[step]):
                place = h if h < SPAN else leaves + h
                block = inc[it, h]
                win[place] = block
                cwin[place] = dot(nbasis[h], block).astype(jnp.bfloat16)

    def near_part(l):
        image = dot(tiles[l], jnp.concatenate([win[near_ref[l, k]] for k in range(near)], axis=0))
        return image

    barrier = pltpu.get_barrier_semaphore()
    for device in (prev_id, next_id):
        pl.semaphore_signal(barrier, inc=1, device_id=device, device_id_type=MESH)
    for j in range(1, group_devs):
        pl.semaphore_signal(barrier, inc=1, device_id=(sub_peer(j), grp), device_id_type=MESH)
    for j in range(1, groups):
        pl.semaphore_signal(barrier, inc=1, device_id=(sub, grp_peer(j)), device_id_type=MESH)

    loads[0].wait()
    for l in range(leaves):
        start = relax_step * rhs_ref[l]
        x_ref[l] = start
        out[0, l] = start.astype(jnp.bfloat16)
    pl.semaphore_wait(barrier, 2 + (group_devs - 1) + (groups - 1))

    for step in range(early):
        to_prev(0, prev_order[step]).start()
        to_next(0, next_order[step]).start()
    for load in loads[1:]:
        load.wait()
    for j in range(1, group_devs):
        dt_copy(j, sub).start()
    basis_copy(0).start()
    basis_copy(1).start()

    total_leaves = leaves * count
    window = leaves + 2 * SPAN
    for l in range(leaves):
        for k in range(near):
            place = near_raw[l, k] - me * leaves + SPAN
            place = jnp.where(place < 0, place + total_leaves, place)
            place = jnp.where(place >= total_leaves, place - total_leaves, place)
            near_ref[l, k] = jnp.minimum(place, window - 1)
        for k in range(nfar):
            place = far_raw[k, l] - me * leaves + SPAN
            place = jnp.where(place < 0, place + total_leaves, place)
            place = jnp.where(place >= total_leaves, place - total_leaves, place)
            far_ref[k, l] = jnp.minimum(place, window - 1)

    dt_all[sub] = dt_ref[0]
    dt_t[...] = flip(dt_ref[0])
    lanes = noise_raw.shape[1]
    pieces = size // lanes
    for l in range(leaves):
        basis_t[l] = flip(basis_ref[l])
        for k in range(nfar):
            far_all[l, :, pl.ds(k * rank, rank)] = lc_ref[l, k]
        far_all[l, :, pl.ds(nfar * rank, rank)] = flip(lt_ref[l])
        for c in range(pieces):
            row = noise_raw[pl.ds(l * pieces + c, 1), :]
            noise_ref[l, pl.ds(c * lanes, lanes), :] = jnp.broadcast_to(row, (probes, lanes)).T
    for j in range(1, group_devs):
        dt_copy(j, lax.rem(sub + group_devs - j, group_devs)).wait_recv()
    for load in tile_loads:
        load.wait()

    def sweep(it, carry):
        for step in range(early, SPAN):
            to_prev(it, prev_order[step]).start()
            to_next(it, next_order[step]).start()
        total = None
        for l in range(leaves):
            block = out[it, l]
            win[SPAN + l] = block
            coef = dot(basis_ref[l], block).astype(jnp.bfloat16)
            cwin[SPAN + l] = coef
            term = dot(lt_ref[l], coef)
            total = term if total is None else total + term
        gath[it, sub] = total.astype(jnp.bfloat16)
        for j in range(1, group_devs):
            gath_copy(it, j, sub).start()

        @pl.when(it == 0)
        def _():
            basis_copy(0).wait_recv()
            basis_copy(1).wait_recv()

        def arrive(steps):
            stage(it, steps)
            for step in steps:
                for l in by_step[step + 1]:
                    image_ref[l] = near_part(l)

        for l in by_step[0]:
            image_ref[l] = near_part(l)
        arrive(range(early))

        for j in range(1, group_devs):
            gath_copy(it, j, lax.rem(sub + group_devs - j, group_devs)).wait_recv()
        for m in range(mid_grp):
            lifted = None
            for s in range(MID_DEVS):
                place = m * MID_DEVS + s
                coef = gath[it, place]
                gath_here[place] = coef
                term = dot(dt_all[place], coef).astype(jnp.bfloat16).astype(jnp.float32)
                lifted = term if lifted is None else lifted + term
            mid[it, grp * mid_grp + m] = lifted.astype(jnp.bfloat16)
        for j in range(1, groups):
            mid_copy(it, j, grp).start()

        dev_total = None
        for k in range(nfdev):
            term = dot(dc_ref[0, k], gath_here[lax.div(fdev_ref[0, k], groups)])
            dev_total = term if dev_total is None else dev_total + term

        arrive(range(early, middle))

        for j in range(1, groups):
            mid_copy(it, j, lax.rem(grp + groups - j, groups)).wait_recv()
        for m in range(groups * mid_grp):
            mid_here[m] = mid[it, m]
        own_mid = sub // MID_DEVS
        field = None
        for k in range(nfmid):
            term = dot(mc_ref[own_mid, k], mid_here[fmid_ref[own_mid, k]])
            field = term if field is None else field + term
        dev_field = (dev_total + dot(dt_t[...], field.astype(jnp.bfloat16))).astype(jnp.bfloat16)

        def finish(batch):
            for l in batch:
                parts = [cwin[far_ref[k, l]] for k in range(nfar)] + [dev_field]
                field_ref[l] = dot(far_all[l], jnp.concatenate(parts, axis=0)).astype(jnp.bfloat16)
            for at in range(0, len(batch), 2):
                pair = batch[at : at + 2]
                for l in pair:
                    image = image_ref[l] + dot(basis_t[l], field_ref[l])
                    old = x_ref[l]
                    image = image + noise_ref[l] * old
                    new = old + relax_step * (rhs_ref[l] - image)
                    x_ref[l] = new
                    out[it + 1, l] = new.astype(jnp.bfloat16)
                if any(l in first or l in last for l in pair):

                    @pl.when(it + 1 < ITERS)
                    def _():
                        for l in pair:
                            if l in first:
                                to_prev(it + 1, l).start()
                            if l in last:
                                to_next(it + 1, l - (leaves - SPAN)).start()

        done = [l for step in range(middle + 1) for l in reversed(by_step[step])]
        finish(sends_first(done))

        @pl.when(it == 0)
        def _():
            for j in range(1, group_devs):
                dt_copy(j, sub).wait_send()
            basis_copy(0).wait_send()
            basis_copy(1).wait_send()

        for j in range(1, group_devs):
            gath_copy(it, j, sub).wait_send()
        for j in range(1, groups):
            mid_copy(it, j, grp).wait_send()
        for h in range(SPAN):
            to_prev(it, h).wait_send()
            to_next(it, h).wait_send()
        arrive(range(middle, SPAN))
        finish(sends_first([l for l in range(leaves) if l not in done]))
        return carry

    lax.fori_loop(0, ITERS, sweep, 0)


def per_device(
    right_side,
    noise_var,
    near_tiles,
    near_index,
    leaf_basis,
    leaf_transfer,
    leaf_coupling,
    far_leaf,
    dev_transfer,
    dev_coupling,
    far_dev,
    mid_coupling,
    far_mid,
):
    leaves, near, size, _ = near_tiles.shape
    probes = right_side.shape[1]
    rank = leaf_basis.shape[1]
    groups = lax.axis_size("grp")
    group_devs = lax.axis_size("sub")
    window = leaves + 2 * SPAN
    all_mids = groups * (group_devs // MID_DEVS)
    bf16, f32, i32 = jnp.bfloat16, jnp.float32, jnp.int32
    dma = pltpu.SemaphoreType.DMA
    operands = [
        near_index,
        far_leaf.T,
        far_dev,
        far_mid,
        right_side.reshape(leaves, size, probes),
        noise_var.reshape(-1, probes),
        leaf_basis,
        leaf_transfer,
        leaf_coupling,
        dev_transfer,
        dev_coupling,
        mid_coupling,
        near_tiles,
    ]
    scratch = [pltpu.SMEM(a.shape, i32) for a in operands[:4]]
    scratch += [pltpu.SMEM(a.shape, i32) for a in operands[:2]]
    scratch += [pltpu.VMEM(a.shape, a.dtype) for a in operands[4:-1]]
    scratch += [pltpu.VMEM((leaves, size, near * size), bf16)]
    scratch += [
        pltpu.VMEM((leaves, size, probes), f32),
        pltpu.VMEM((leaves, size, rank), bf16),
        pltpu.VMEM((leaves, rank, (far_leaf.shape[1] + 1) * rank), bf16),
        pltpu.VMEM((leaves, rank, probes), bf16),
        pltpu.VMEM((rank, rank), bf16),
        pltpu.VMEM((window, rank, probes), bf16),
        pltpu.VMEM((2 * SPAN, rank, size), bf16),
        pltpu.VMEM((group_devs, rank, rank), bf16),
        pltpu.VMEM((group_devs, rank, probes), bf16),
        pltpu.VMEM((all_mids, rank, probes), bf16),
        pltpu.VMEM((leaves, size, probes), f32),
        pltpu.VMEM((window, size, probes), bf16),
        pltpu.VMEM((ITERS + 1, leaves, size, probes), bf16),
        pltpu.VMEM((ITERS, 2 * SPAN, size, probes), bf16),
        pltpu.VMEM((ITERS, group_devs, rank, probes), bf16),
        pltpu.VMEM((ITERS, all_mids, rank, probes), bf16),
        dma((12,)),
        dma((leaves, near)),
        dma((ITERS, 2, SPAN)),
        dma((ITERS, 2, SPAN)),
        dma((2,)),
        dma((2,)),
        dma((group_devs,)),
        dma((group_devs,)),
        dma((ITERS, group_devs)),
        dma((ITERS, group_devs)),
        dma((ITERS, groups)),
        dma((ITERS, groups)),
    ]
    result = pl.pallas_call(
        functools.partial(kernel, groups, group_devs),
        out_shape=jax.ShapeDtypeStruct((leaves, size, probes), f32),
        in_specs=[pl.BlockSpec(memory_space=pl.ANY)] * len(operands),
        out_specs=pl.BlockSpec(memory_space=pltpu.VMEM),
        scratch_shapes=scratch,
        compiler_params=pltpu.CompilerParams(
            collective_id=0, has_side_effects=True, vmem_limit_bytes=56 * 1024 * 1024
        ),
    )(*operands)
    return result.reshape(leaves * size, probes)


def solution(mesh):
    return jax.shard_map(
        per_device,
        mesh=mesh,
        in_specs=(
            P(("sub", "grp"), None),
            P(("sub", "grp")),
            P(("sub", "grp"), None, None, None),
            P(("sub", "grp"), None),
            P(("sub", "grp"), None, None),
            P(("sub", "grp"), None, None),
            P(("sub", "grp"), None, None, None),
            P(("sub", "grp"), None),
            P(("sub", "grp"), None, None),
            P(("sub", "grp"), None, None, None),
            P(("sub", "grp"), None),
            P("grp", None, None, None),
            P("grp", None),
        ),
        out_specs=P(("sub", "grp"), None),
        check_vma=False,
    )
```

```python
import functools

import jax
import jax.numpy as jnp
from jax import lax
from jax.experimental import pallas as pl
from jax.experimental.pallas import tpu as pltpu
from jax.sharding import PartitionSpec as P

SPAN = 6
ITERS = 4
MID_DEVS = 8
MESH = pl.DeviceIdType.MESH


relax_step = 0.3


def dot(a, b):
    return jnp.dot(a, b, preferred_element_type=jnp.float32)


def flip(a):
    return a.astype(jnp.float32).T.astype(jnp.bfloat16)


def kernel(
    groups,
    group_devs,
    near_hbm,
    far_hbm,
    fdev_hbm,
    fmid_hbm,
    rhs_hbm,
    noise_hbm,
    basis_hbm,
    lt_hbm,
    lc_hbm,
    dt_hbm,
    dc_hbm,
    mc_hbm,
    tiles_hbm,
    x_ref,
    near_raw,
    far_raw,
    fdev_ref,
    fmid_ref,
    near_ref,
    far_ref,
    rhs_ref,
    noise_raw,
    basis_ref,
    lt_ref,
    lc_ref,
    dt_ref,
    dc_ref,
    mc_ref,
    tiles,
    noise_ref,
    basis_t,
    far_all,
    field_ref,
    dt_t,
    cwin,
    nbasis,
    dt_all,
    gath_here,
    mid_here,
    image_ref,
    win,
    out,
    inc,
    gath,
    mid,
    in_sem,
    tile_sem,
    halo_send,
    halo_recv,
    nb_send,
    nb_recv,
    dt_send,
    dt_recv,
    g_send,
    g_recv,
    m_send,
    m_recv,
):
    leaves, size, probes = rhs_ref.shape
    rank = basis_ref.shape[1]
    near = near_ref.shape[1]
    nfar = far_ref.shape[0]
    nfdev = fdev_ref.shape[1]
    nfmid = fmid_ref.shape[1]
    mid_grp = group_devs // MID_DEVS
    count = groups * group_devs
    sub = lax.axis_index("sub")
    grp = lax.axis_index("grp")
    me = sub * groups + grp
    nxt = lax.rem(me + 1, count)
    prv = lax.rem(me + count - 1, count)
    next_id = (nxt // groups, lax.rem(nxt, groups))
    prev_id = (prv // groups, lax.rem(prv, groups))

    operands = [
        (rhs_hbm, rhs_ref),
        (basis_hbm, basis_ref),
        (dt_hbm, dt_ref),
        (lt_hbm, lt_ref),
        (near_hbm, near_raw),
        (far_hbm, far_raw),
        (fdev_hbm, fdev_ref),
        (fmid_hbm, fmid_ref),
        (noise_hbm, noise_raw),
        (lc_hbm, lc_ref),
        (dc_hbm, dc_ref),
        (mc_hbm, mc_ref),
    ]
    loads = [
        pltpu.make_async_copy(src, dst, in_sem.at[i]) for i, (src, dst) in enumerate(operands)
    ]
    for load in loads:
        load.start()
    tile_loads = [
        pltpu.make_async_copy(
            tiles_hbm.at[l, k], tiles.at[l, :, pl.ds(k * size, size)], tile_sem.at[l, k]
        )
        for l in range(leaves)
        for k in range(near)
    ]

    def sub_peer(j):
        return lax.rem(sub + j, group_devs)

    def grp_peer(j):
        return lax.rem(grp + j, groups)

    def remote(src, dst, send, recv, device):
        return pltpu.make_async_remote_copy(
            src_ref=src,
            dst_ref=dst,
            send_sem=send,
            recv_sem=recv,
            device_id=device,
            device_id_type=MESH,
        )

    def to_prev(it, h):
        return remote(
            out.at[it, h],
            inc.at[it, SPAN + h],
            halo_send.at[it, 0, h],
            halo_recv.at[it, 0, h],
            prev_id,
        )

    def to_next(it, h):
        return remote(
            out.at[it, leaves - SPAN + h],
            inc.at[it, h],
            halo_send.at[it, 1, h],
            halo_recv.at[it, 1, h],
            next_id,
        )

    def basis_copy(side):
        if side == 0:
            src, dst, device = basis_ref.at[pl.ds(0, SPAN)], nbasis.at[pl.ds(SPAN, SPAN)], prev_id
        else:
            src, dst, device = (
                basis_ref.at[pl.ds(leaves - SPAN, SPAN)],
                nbasis.at[pl.ds(0, SPAN)],
                next_id,
            )
        return remote(src, dst, nb_send.at[side], nb_recv.at[side], device)

    def dt_copy(j, owner):
        return remote(
            dt_ref.at[0], dt_all.at[owner], dt_send.at[j], dt_recv.at[j], (sub_peer(j), grp)
        )

    def gath_copy(it, j, owner):
        block = gath.at[it, owner]
        return remote(block, block, g_send.at[it, j], g_recv.at[it, j], (sub_peer(j), grp))

    def mid_copy(it, j, owner):
        block = mid.at[it, pl.ds(owner * mid_grp, mid_grp)]
        return remote(block, block, m_send.at[it, j], m_recv.at[it, j], (sub, grp_peer(j)))

    early = SPAN // 2
    middle = SPAN - 1
    prev_order = list(range(SPAN))
    next_order = list(range(SPAN - 1, -1, -1))
    first = prev_order[:early]
    last = [leaves - SPAN + h for h in next_order[:early]]

    def steps_needed(l):
        return min(SPAN, max(0, SPAN - l, l + SPAN - leaves + 1))

    by_step = [[l for l in range(leaves) if steps_needed(l) == n] for n in range(SPAN + 1)]

    def sends_first(batch):
        return sorted(batch, key=lambda l: (l not in first and l not in last, l))

    def stage(it, steps):
        for step in steps:
            to_next(it, next_order[step]).wait_recv()
            to_prev(it, prev_order[step]).wait_recv()
        for step in steps:
            for h in (next_order[step], SPAN + prev_order[step]):
                place = h if h < SPAN else leaves + h
                block = inc[it, h]
                win[place] = block
                cwin[place] = dot(nbasis[h], block).astype(jnp.bfloat16)

    def near_part(l):
        image = dot(tiles[l], jnp.concatenate([win[near_ref[l, k]] for k in range(near)], axis=0))
        return image

    barrier = pltpu.get_barrier_semaphore()
    for device in (prev_id, next_id):
        pl.semaphore_signal(barrier, inc=1, device_id=device, device_id_type=MESH)
    for j in range(1, group_devs):
        pl.semaphore_signal(barrier, inc=1, device_id=(sub_peer(j), grp), device_id_type=MESH)
    for j in range(1, groups):
        pl.semaphore_signal(barrier, inc=1, device_id=(sub, grp_peer(j)), device_id_type=MESH)

    loads[0].wait()
    for l in range(leaves):
        start = relax_step * rhs_ref[l]
        x_ref[l] = start
        out[0, l] = start.astype(jnp.bfloat16)
    pl.semaphore_wait(barrier, 2 + (group_devs - 1) + (groups - 1))

    for step in range(early):
        to_prev(0, prev_order[step]).start()
        to_next(0, next_order[step]).start()
    for load in tile_loads:
        load.start()
    for load in loads[1:]:
        load.wait()
    for j in range(1, group_devs):
        dt_copy(j, sub).start()
    basis_copy(0).start()
    basis_copy(1).start()

    total_leaves = leaves * count
    window = leaves + 2 * SPAN
    for l in range(leaves):
        for k in range(near):
            place = near_raw[l, k] - me * leaves + SPAN
            place = jnp.where(place < 0, place + total_leaves, place)
            place = jnp.where(place >= total_leaves, place - total_leaves, place)
            near_ref[l, k] = jnp.minimum(place, window - 1)
        for k in range(nfar):
            place = far_raw[k, l] - me * leaves + SPAN
            place = jnp.where(place < 0, place + total_leaves, place)
            place = jnp.where(place >= total_leaves, place - total_leaves, place)
            far_ref[k, l] = jnp.minimum(place, window - 1)

    dt_all[sub] = dt_ref[0]
    dt_t[...] = flip(dt_ref[0])
    lanes = noise_raw.shape[1]
    pieces = size // lanes
    for l in range(leaves):
        basis_t[l] = flip(basis_ref[l])
        for k in range(nfar):
            far_all[l, :, pl.ds(k * rank, rank)] = lc_ref[l, k]
        far_all[l, :, pl.ds(nfar * rank, rank)] = flip(lt_ref[l])
        for c in range(pieces):
            row = noise_raw[pl.ds(l * pieces + c, 1), :]
            noise_ref[l, pl.ds(c * lanes, lanes), :] = jnp.broadcast_to(row, (probes, lanes)).T
    for j in range(1, group_devs):
        dt_copy(j, lax.rem(sub + group_devs - j, group_devs)).wait_recv()
    for load in tile_loads:
        load.wait()

    def sweep(it, carry):
        total = None
        for l in range(leaves):
            block = out[it, l]
            win[SPAN + l] = block
            coef = dot(basis_ref[l], block).astype(jnp.bfloat16)
            cwin[SPAN + l] = coef
            term = dot(lt_ref[l], coef)
            total = term if total is None else total + term
        gath[it, sub] = total.astype(jnp.bfloat16)
        for j in range(1, group_devs):
            gath_copy(it, j, sub).start()
        for step in range(early, middle):
            to_prev(it, prev_order[step]).start()
            to_next(it, next_order[step]).start()

        @pl.when(it == 0)
        def _():
            basis_copy(0).wait_recv()
            basis_copy(1).wait_recv()

        def arrive(steps):
            stage(it, steps)
            for step in steps:
                for l in by_step[step + 1]:
                    image_ref[l] = near_part(l)

        for l in by_step[0]:
            image_ref[l] = near_part(l)
        arrive(range(early))

        for j in range(1, group_devs):
            gath_copy(it, j, lax.rem(sub + group_devs - j, group_devs)).wait_recv()
        for m in range(mid_grp):
            lifted = None
            for s in range(MID_DEVS):
                place = m * MID_DEVS + s
                coef = gath[it, place]
                gath_here[place] = coef
                term = dot(dt_all[place], coef).astype(jnp.bfloat16).astype(jnp.float32)
                lifted = term if lifted is None else lifted + term
            mid[it, grp * mid_grp + m] = lifted.astype(jnp.bfloat16)
        for j in range(1, groups):
            mid_copy(it, j, grp).start()
        for step in range(middle, SPAN):
            to_prev(it, prev_order[step]).start()
            to_next(it, next_order[step]).start()

        dev_total = None
        for k in range(nfdev):
            term = dot(dc_ref[0, k], gath_here[lax.div(fdev_ref[0, k], groups)])
            dev_total = term if dev_total is None else dev_total + term

        arrive(range(early, middle))

        for j in range(1, groups):
            mid_copy(it, j, lax.rem(grp + groups - j, groups)).wait_recv()
        for m in range(groups * mid_grp):
            mid_here[m] = mid[it, m]
        own_mid = sub // MID_DEVS
        field = None
        for k in range(nfmid):
            term = dot(mc_ref[own_mid, k], mid_here[fmid_ref[own_mid, k]])
            field = term if field is None else field + term
        dev_field = (dev_total + dot(dt_t[...], field.astype(jnp.bfloat16))).astype(jnp.bfloat16)

        def finish(batch):
            for l in batch:
                parts = [cwin[far_ref[k, l]] for k in range(nfar)] + [dev_field]
                field_ref[l] = dot(far_all[l], jnp.concatenate(parts, axis=0)).astype(jnp.bfloat16)
            for at in range(0, len(batch), 2):
                pair = batch[at : at + 2]
                for l in pair:
                    image = image_ref[l] + dot(basis_t[l], field_ref[l])
                    old = x_ref[l]
                    image = image + noise_ref[l] * old
                    new = old + relax_step * (rhs_ref[l] - image)
                    x_ref[l] = new
                    out[it + 1, l] = new.astype(jnp.bfloat16)
                if any(l in first or l in last for l in pair):

                    @pl.when(it + 1 < ITERS)
                    def _():
                        for l in pair:
                            if l in first:
                                to_prev(it + 1, l).start()
                            if l in last:
                                to_next(it + 1, l - (leaves - SPAN)).start()

        done = [l for step in range(middle + 1) for l in reversed(by_step[step])]
        finish(sends_first(done))

        @pl.when(it == 0)
        def _():
            for j in range(1, group_devs):
                dt_copy(j, sub).wait_send()
            basis_copy(0).wait_send()
            basis_copy(1).wait_send()

        for j in range(1, group_devs):
            gath_copy(it, j, sub).wait_send()
        for j in range(1, groups):
            mid_copy(it, j, grp).wait_send()
        for h in range(SPAN):
            to_prev(it, h).wait_send()
            to_next(it, h).wait_send()
        arrive(range(middle, SPAN))
        finish(sends_first([l for l in range(leaves) if l not in done]))
        return carry

    lax.fori_loop(0, ITERS, sweep, 0)


def per_device(
    right_side,
    noise_var,
    near_tiles,
    near_index,
    leaf_basis,
    leaf_transfer,
    leaf_coupling,
    far_leaf,
    dev_transfer,
    dev_coupling,
    far_dev,
    mid_coupling,
    far_mid,
):
    leaves, near, size, _ = near_tiles.shape
    probes = right_side.shape[1]
    rank = leaf_basis.shape[1]
    groups = lax.axis_size("grp")
    group_devs = lax.axis_size("sub")
    window = leaves + 2 * SPAN
    all_mids = groups * (group_devs // MID_DEVS)
    bf16, f32, i32 = jnp.bfloat16, jnp.float32, jnp.int32
    dma = pltpu.SemaphoreType.DMA
    operands = [
        near_index,
        far_leaf.T,
        far_dev,
        far_mid,
        right_side.reshape(leaves, size, probes),
        noise_var.reshape(-1, probes),
        leaf_basis,
        leaf_transfer,
        leaf_coupling,
        dev_transfer,
        dev_coupling,
        mid_coupling,
        near_tiles,
    ]
    scratch = [pltpu.SMEM(a.shape, i32) for a in operands[:4]]
    scratch += [pltpu.SMEM(a.shape, i32) for a in operands[:2]]
    scratch += [pltpu.VMEM(a.shape, a.dtype) for a in operands[4:-1]]
    scratch += [pltpu.VMEM((leaves, size, near * size), bf16)]
    scratch += [
        pltpu.VMEM((leaves, size, probes), f32),
        pltpu.VMEM((leaves, size, rank), bf16),
        pltpu.VMEM((leaves, rank, (far_leaf.shape[1] + 1) * rank), bf16),
        pltpu.VMEM((leaves, rank, probes), bf16),
        pltpu.VMEM((rank, rank), bf16),
        pltpu.VMEM((window, rank, probes), bf16),
        pltpu.VMEM((2 * SPAN, rank, size), bf16),
        pltpu.VMEM((group_devs, rank, rank), bf16),
        pltpu.VMEM((group_devs, rank, probes), bf16),
        pltpu.VMEM((all_mids, rank, probes), bf16),
        pltpu.VMEM((leaves, size, probes), f32),
        pltpu.VMEM((window, size, probes), bf16),
        pltpu.VMEM((ITERS + 1, leaves, size, probes), bf16),
        pltpu.VMEM((ITERS, 2 * SPAN, size, probes), bf16),
        pltpu.VMEM((ITERS, group_devs, rank, probes), bf16),
        pltpu.VMEM((ITERS, all_mids, rank, probes), bf16),
        dma((12,)),
        dma((leaves, near)),
        dma((ITERS, 2, SPAN)),
        dma((ITERS, 2, SPAN)),
        dma((2,)),
        dma((2,)),
        dma((group_devs,)),
        dma((group_devs,)),
        dma((ITERS, group_devs)),
        dma((ITERS, group_devs)),
        dma((ITERS, groups)),
        dma((ITERS, groups)),
    ]
    result = pl.pallas_call(
        functools.partial(kernel, groups, group_devs),
        out_shape=jax.ShapeDtypeStruct((leaves, size, probes), f32),
        in_specs=[pl.BlockSpec(memory_space=pl.ANY)] * len(operands),
        out_specs=pl.BlockSpec(memory_space=pltpu.VMEM),
        scratch_shapes=scratch,
        compiler_params=pltpu.CompilerParams(
            collective_id=0, has_side_effects=True, vmem_limit_bytes=56 * 1024 * 1024
        ),
    )(*operands)
    return result.reshape(leaves * size, probes)


def solution(mesh):
    return jax.shard_map(
        per_device,
        mesh=mesh,
        in_specs=(
            P(("sub", "grp"), None),
            P(("sub", "grp")),
            P(("sub", "grp"), None, None, None),
            P(("sub", "grp"), None),
            P(("sub", "grp"), None, None),
            P(("sub", "grp"), None, None),
            P(("sub", "grp"), None, None, None),
            P(("sub", "grp"), None),
            P(("sub", "grp"), None, None),
            P(("sub", "grp"), None, None, None),
            P(("sub", "grp"), None),
            P("grp", None, None, None),
            P("grp", None),
        ),
        out_specs=P(("sub", "grp"), None),
        check_vma=False,
    )
```
